256 devices in a mesh: grp: 2 (over z_lo), seq: 16 (over z_hi, x), dp: 8 (over y, core).
Axes of the slice: x: 4, y: 4, z: 8 (z_hi: 4, z_lo: 2; z = z_hi * 2 + z_lo), core: 2. Of those that a mesh axis runs over, the one named last changes fastest.
Arguments:
- features: bfloat16 [16, 8, 16, 16, 512], P(('grp', 'dp'), None, 'seq'), may hold values from -6 to 6
- conv_weight: bfloat16 [3, 3, 512, 4], replicated, may hold values from -0.09375 to 0.09375
- conv_bias: float32 [4], replicated, may hold values from -3 to 3
- noise: bfloat16 [16, 8, 16, 16, 4], P(('grp', 'dp'), None, 'seq'), may hold values from -6 to 6
- timestep: int32 [16], P(('grp', 'dp')), may hold values from 0 to 999
- camera: int32 [16, 8], P(('grp', 'dp')), may hold values from 0 to 63
- view_table: bfloat16 [64, 1152], replicated, may hold values from -6 to 6
- latent_proj: bfloat16 [4, 1152], replicated, may hold values from -3 to 3
- hidden: bfloat16 [16, 8, 16, 16, 1152], P(('grp', 'dp'), None, 'seq'), may hold values from -8 to 8
- ln_gain: float32 [1152], replicated, may hold values from 0.1 to 1.9
- qkv_weight: bfloat16 [1152, 3456], replicated, may hold values from -1 to 1
- cotangent: bfloat16 [16, 8, 16, 16, 1152], P(('grp', 'dp'), None, None, None, 'seq'), may hold values from -6 to 6
Outputs:
- attended: bfloat16 [16, 8, 16, 16, 1152], P(('grp', 'dp'), None, None, None, 'seq')
- hidden_grad: bfloat16 [16, 8, 16, 16, 1152], P(('grp', 'dp'), None, 'seq')
- weight_grad: float32 [16, 1152, 216], P('seq', ('grp', 'dp'))
The draws below stay inside these ranges and needn't reach their ends.
All inputs are finite; a program needn't handle non-finite values.
Results may differ from the reference program's by a relative error of at most 0.022.
Values may be sent and summed in bfloat16 or wider, within the bound.
A program may use at most 192 MiB of HBM per device.

```python
import math
import jax
import jax.numpy as jnp
from jax import lax

D = 1152
H = 16
HD = 72
C = 512
LC = 4
NCAM = 64
TSTEPS = 1000
VIEWS = 8
LW = 16
SCENES = 16
LH = 16
NK = 2048


def draw_hidden(key, part):
    key = jax.random.fold_in(key, 11)
    base_key = jax.random.fold_in(key, 0)
    shape = (SCENES, VIEWS, LH, LW, D)
    values = jnp.clip(jax.random.normal(base_key, shape, jnp.float32), -6.0, 6.0)
    return values.astype(jnp.bfloat16)


def draw_qkv_weight(key, part):
    key = jax.random.fold_in(key, 12)
    base_key = jax.random.fold_in(key, 0)
    values = jnp.clip(jax.random.normal(base_key, (D, 3 * D), jnp.float32), -6.0, 6.0) / math.sqrt(D)
    return values.astype(jnp.bfloat16)


def set_ends(array, rng, low, top_value):
    longest = array.shape.index(max(array.shape))
    spots = []
    for shift in (0, 1):
        where = [jax.random.randint(jax.random.fold_in(rng, axis), (), 0, length) for axis, length in enumerate(array.shape)]
        where[longest] = (where[longest] + shift) % array.shape[longest]
        spots.append(tuple(where))
    return array.at[spots[0]].set(low).at[spots[1]].set(top_value)


def level_of(own_key, shape, shards, smallest, top_value):
    factor_of = 1.0
    for position, blocks in shards:
        steps = jax.random.uniform(jax.random.fold_in(jax.random.fold_in(own_key, 6), position), (blocks,), jnp.float32, smallest / len(shards), top_value / len(shards))
        factor_of = factor_of * jnp.repeat(jnp.exp(steps), shape[position] // blocks).reshape((-1,) + (1,) * (len(shape) - 1 - position))
    return factor_of


def centred(stream_key, extent, deviation, bound, shards=(), kind=jnp.bfloat16):
    values = jax.random.normal(stream_key, extent, jnp.float32) * deviation
    if len(shards) > 0:
        values = level_of(stream_key, extent, shards, -0.22, 0.18) * values
    return jnp.clip(values, min=-bound, max=bound).astype(kind)


def setup_inputs(seed: int = 0) -> dict:
    key_of = jax.random.split(jax.random.key(seed), 13)
    return {
        "features": centred(key_of[0], (SCENES, VIEWS, LH, LW, C), 1.0, 6.0, ((0, 16), (2, 16))),
        "conv_weight": centred(key_of[1], (3, 3, C, LC), (9 * C) ** -0.5, 0.09375),
        "conv_bias": centred(key_of[2], (LC,), 1.0, 3.0, (), jnp.float32),
        "noise": centred(key_of[3], (SCENES, VIEWS, LH, LW, LC), 1.0, 6.0, ((0, 16), (2, 16))),
        "timestep": set_ends(jax.random.randint(key_of[4], (SCENES,), 0, TSTEPS), jax.random.fold_in(key_of[4], 1), 0, TSTEPS - 1).astype(jnp.int32),
        "camera": set_ends(jax.random.randint(key_of[5], (SCENES, VIEWS), 0, NCAM), jax.random.fold_in(key_of[5], 1), 0, NCAM - 1).astype(jnp.int32),
        "view_table": centred(key_of[6], (NCAM, D), 1.0, 6.0),
        "latent_proj": centred(key_of[7], (LC, D), LC ** -0.5, 3.0),
        "hidden": draw_hidden(jax.random.fold_in(key_of[12], 71), 0),
        "ln_gain": jnp.clip(1.0 + 0.18 * jax.random.normal(key_of[9], (D,), jnp.float32), 0.1, 1.9),
        "qkv_weight": draw_qkv_weight(jax.random.fold_in(key_of[12], 71), 0),
        "cotangent": centred(key_of[11], (SCENES, VIEWS, LH, LW, D), 1.0, 6.0, ((0, 16), (4, 16))),
    }


def encode_latent(rimmed, conv_weight, conv_bias):
    activated = jax.nn.silu(rimmed.astype(jnp.float32))
    padded = jnp.pad(activated, ((0, 0), (0, 0), (0, 0), (1, 1), (0, 0)))
    rows_out = padded.shape[2] - 2
    cols_out = padded.shape[3] - 2
    latent = jnp.zeros(padded.shape[:2] + (rows_out, cols_out, conv_weight.shape[3]), jnp.float32)
    latent = latent + conv_bias.astype(jnp.float32)
    for row_tap in range(3):
        for col_tap in range(3):
            window = padded[:, :, row_tap:row_tap + rows_out, col_tap:col_tap + cols_out, :]
            latent = latent + jnp.einsum('svhwc,co->svhwo', window, conv_weight[row_tap, col_tap].astype(jnp.float32), precision=lax.Precision.HIGHEST)
    return latent

def layer_input(latent, noise, timestep, camera, view_table, latent_proj, hidden):
    level = timestep.astype(jnp.float32) / TSTEPS
    signal = jnp.cos((level + 0.008) / 1.008 * (math.pi / 2.0)) ** 2
    keep_scale = jnp.sqrt(signal)[:, None, None, None, None]
    noise_scale = jnp.sqrt(1.0 - signal)[:, None, None, None, None]
    noisy = keep_scale * latent + noise_scale * noise.astype(jnp.float32)
    onehot = (camera[..., None] == jnp.arange(view_table.shape[0], dtype=jnp.int32)).astype(jnp.float32)
    view_embed = jnp.einsum('svn,nd->svd', onehot, view_table.astype(jnp.float32), precision=lax.Precision.HIGHEST)
    injected = jnp.einsum('svhwc,cd->svhwd', noisy, latent_proj.astype(jnp.float32), precision=lax.Precision.HIGHEST)
    return hidden.astype(jnp.float32) + injected + view_embed[:, :, None, None, :]

def normalize(inputs, ln_gain):
    mean_value = lax.optimization_barrier(jnp.mean(inputs, -1, keepdims=True))
    centered = inputs - mean_value
    variance = lax.optimization_barrier(jnp.mean(centered * centered, -1, keepdims=True))
    inverse = lax.rsqrt(variance + 1e-06)
    unit = centered * inverse
    return (unit, inverse, (unit * ln_gain).astype(jnp.bfloat16))

def norm_backward(normed_grad, unit, inverse, ln_gain):
    scaled = normed_grad * ln_gain
    first = lax.optimization_barrier(jnp.mean(scaled, -1, keepdims=True))
    second = lax.optimization_barrier(jnp.mean(scaled * unit, -1, keepdims=True))
    return inverse * (scaled - first - unit * second)

def attend(queries, keys, values, upstream):
    count = queries.shape[0]
    block = min(512, count)
    nblocks = count // block
    scale = keys.shape[1] ** (-0.5)

    def step(carry, item):
        key_grad, value_grad = carry
        query_block, up_block = item
        scores = jnp.dot(query_block, keys.T, preferred_element_type=jnp.float32) * scale
        highest = lax.optimization_barrier(jnp.max(scores, -1, keepdims=True))
        weights = jnp.exp(scores - highest)
        probs = weights / lax.optimization_barrier(jnp.sum(weights, -1, keepdims=True))
        probs_low = probs.astype(jnp.bfloat16)
        output = jnp.dot(probs_low, values, preferred_element_type=jnp.float32).astype(jnp.bfloat16)
        prob_grad = jnp.dot(up_block, values.T, preferred_element_type=jnp.float32)
        row_total = lax.optimization_barrier(jnp.sum(probs * prob_grad, -1, keepdims=True))
        score_grad = (probs * (prob_grad - row_total) * scale).astype(jnp.bfloat16)
        query_grad = jnp.dot(score_grad, keys, preferred_element_type=jnp.float32)
        key_grad = key_grad + jnp.dot(score_grad.T, query_block, preferred_element_type=jnp.float32)
        value_grad = value_grad + jnp.dot(probs_low.T, up_block, preferred_element_type=jnp.float32)
        return ((key_grad, value_grad), (output, query_grad))
    zeros = jnp.zeros(keys.shape, jnp.float32)
    blocks_in = (queries.reshape(nblocks, block, -1), upstream.reshape(nblocks, block, -1))
    (key_grad, value_grad), (outputs, query_grads) = lax.scan(step, (zeros, zeros), blocks_in)
    return (outputs.reshape(count, -1), query_grads.reshape(count, -1), key_grad, value_grad)

def per_head(item):
    triple, upstream = item
    return attend(triple[0], triple[1], triple[2], upstream)

def reference(features, conv_weight, conv_bias, noise, timestep, camera, view_table, latent_proj, hidden, ln_gain, qkv_weight, cotangent):
    rimmed = jnp.pad(features, ((0, 0), (0, 0), (1, 1), (0, 0), (0, 0)))
    latent = encode_latent(rimmed, conv_weight, conv_bias)
    inputs = layer_input(latent, noise, timestep, camera, view_table, latent_proj, hidden)
    unit, inverse, normed = normalize(inputs, ln_gain)
    flat_normed = normed.reshape(-1, D)
    projected = jnp.dot(flat_normed, qkv_weight, preferred_element_type=jnp.float32).astype(jnp.bfloat16)
    triples = projected.reshape(SCENES, NK, 3, H, HD).transpose(0, 3, 2, 1, 4).reshape(SCENES * H, 3, NK, HD)
    upstream = cotangent.reshape(SCENES, NK, H, HD).transpose(0, 2, 1, 3).reshape(SCENES * H, NK, HD)
    outputs, query_grad, key_grad, value_grad = lax.map(per_head, (triples, upstream))
    attended = outputs.reshape(SCENES, H, NK, HD).transpose(0, 2, 1, 3).reshape(SCENES, VIEWS, LH, LW, D)
    grads = jnp.stack([query_grad, key_grad, value_grad], 1).astype(jnp.bfloat16)
    grads = grads.reshape(SCENES, H, 3, NK, HD).transpose(0, 3, 2, 1, 4).reshape(SCENES * NK, 3 * D)
    full_grad = jnp.dot(flat_normed.T, grads, preferred_element_type=jnp.float32)
    weight_grad = full_grad.reshape(D, 3, H, HD).transpose(2, 0, 1, 3).reshape(H, D, 3 * HD)
    normed_grad = jnp.dot(grads, qkv_weight.T, preferred_element_type=jnp.float32).reshape(inputs.shape)
    hidden_grad = norm_backward(normed_grad, unit, inverse, ln_gain).astype(jnp.bfloat16)
    return (attended, hidden_grad, weight_grad)
```

```python
import functools
import math

import jax
import jax.numpy as jnp
from jax import lax
from jax.experimental import pallas as pl
from jax.experimental.pallas import tpu as pltpu
from jax.sharding import PartitionSpec as P

MESH = pl.DeviceIdType.MESH
F32 = jnp.float32
BF16 = jnp.bfloat16
TOK = 128
VIEWS = 8
COLS = 16
ROWS = 16
D = 1152
HD = 72
NX = 4
NZ = 4
PACK = 224
WIN = 384
Q_SCALE = math.log2(math.e) / math.sqrt(HD)
QB = 256
NQ = 8


def dot(a, b):
    return jnp.dot(a, b, preferred_element_type=F32)


def remote(src, dst, send, recv, device):
    return pltpu.make_async_remote_copy(
        src_ref=src,
        dst_ref=dst,
        send_sem=send,
        recv_sem=recv,
        device_id=device,
        device_id_type=MESH,
    )


def project_kernel(
    tstep,
    cam,
    bias,
    feat,
    w72,
    noise,
    table,
    latp,
    hid,
    gain,
    w_hbm,
    qkv_out,
    norm_out,
    unit_out,
    inv_out,
    halo_send,
    halo_recv,
    ag,
    win,
    pt,
    sendbuf,
    w_sem,
    out_sem,
    hs_sem,
    hr_sem,
    zs_sem,
    zr_sem,
    xs_sem,
    xr_sem,
    own_sem,
):
    me = lax.axis_index("seq")
    z = me // NX
    x = lax.rem(me, NX)

    def at(zz, xx):
        return {"seq": lax.rem(zz + NZ, NZ) * NX + lax.rem(xx + NX, NX)}

    up = {"seq": lax.rem(me + 1, NX * NZ)}
    down = {"seq": lax.rem(me + NX * NZ - 1, NX * NZ)}
    z_up, z_down = at(z + 1, x), at(z - 1, x)
    peers = [up, down, z_up, z_down] + [at(z, x + d) for d in range(1, NX)]
    barrier = pltpu.get_barrier_semaphore()
    for peer in peers:
        pl.semaphore_signal(barrier, inc=1, device_id=peer, device_id_type=MESH)

    w_copies = []
    for t in range(3):
        start = pl.multiple_of(t * D + z * 256, 128)
        copy = pltpu.make_async_copy(
            w_hbm.at[:, pl.ds(start, WIN)], win.at[:, pl.ds(t * WIN, WIN)], w_sem.at[t]
        )
        copy.start()
        w_copies.append(copy)

    f = feat[...].astype(F32)
    act = (f / (1.0 + jnp.exp(-f))).astype(BF16)
    taps = lax.dot_general(w72[...], act, (((1,), (1,)), ((), ())), preferred_element_type=F32)
    lane = lax.rem(lax.broadcasted_iota(jnp.int32, (8, TOK), 1), COLS)
    part = []
    for r in range(3):
        left = pltpu.roll(taps[r * 24 : r * 24 + 8], 1, 1)
        mid = taps[r * 24 + 8 : r * 24 + 16]
        right = pltpu.roll(taps[r * 24 + 16 : r * 24 + 24], TOK - 1, 1)
        part.append(mid + jnp.where(lane == 0, 0.0, left) + jnp.where(lane == COLS - 1, 0.0, right))
    halo_send[0] = part[0]
    halo_send[1] = part[2]
    pl.semaphore_wait(barrier, len(peers))
    halo_up = remote(halo_send.at[0], halo_recv.at[0], hs_sem.at[0], hr_sem.at[0], up)
    halo_down = remote(halo_send.at[1], halo_recv.at[1], hs_sem.at[1], hr_sem.at[1], down)
    halo_up.start()
    halo_down.start()

    node = lax.broadcasted_iota(jnp.int32, (VIEWS, 64), 1)
    view = lax.broadcasted_iota(jnp.int32, (VIEWS, 64), 0)
    picked = jnp.zeros((VIEWS, 64), jnp.int32)
    for v in range(VIEWS):
        picked = jnp.where(view == v, cam[v], picked)
    onehot = jnp.where(node == picked, 1.0, 0.0).astype(BF16)
    embed = dot(onehot, table[...])
    base = hid[...].astype(F32).reshape(VIEWS, COLS, D) + embed[:, None, :]
    base = base.reshape(TOK, D)

    level = jnp.full((8, TOK), tstep[0], jnp.int32).astype(F32) / 1000.0
    cosine = jnp.cos((level + 0.008) / 1.008 * (math.pi / 2.0))
    signal = cosine * cosine
    keep = jnp.sqrt(signal)
    fade = jnp.sqrt(1.0 - signal)

    row = lax.broadcasted_iota(jnp.int32, (8, TOK), 0)
    bias_rows = jnp.zeros((8, TOK), F32)
    for c in range(4):
        bias_rows = jnp.where(row == c, bias[c], bias_rows)
    own = part[1] + bias_rows
    halo_up.wait_recv()
    halo_down.wait_recv()
    own = own + jnp.where(me > 0, halo_recv[0], 0.0)
    own = own + jnp.where(me < NX * NZ - 1, halo_recv[1], 0.0)
    latent = jnp.transpose(own * keep)
    noisy = latent[:, 0:4] + noise[...].astype(F32) * fade[0:1, 0:1]
    inputs = base
    for c in range(4):
        inputs = inputs + noisy[:, c : c + 1] * latp[c : c + 1, :].astype(F32)

    mean = jnp.mean(inputs, -1, keepdims=True)
    centered = inputs - mean
    variance = jnp.mean(centered * centered, -1, keepdims=True)
    inverse = lax.rsqrt(variance + 1e-06)
    unit = centered * inverse
    ag[0] = (unit * gain[...]).astype(BF16)
    send_up = remote(ag.at[0], ag.at[1], zs_sem.at[0], zr_sem.at[0], z_up)
    send_down = remote(ag.at[0], ag.at[3], zs_sem.at[1], zr_sem.at[1], z_down)
    send_up.start()
    send_down.start()
    unit_out[...] = unit
    inv_out[...] = jnp.broadcast_to(inverse, (TOK, 128))

    for copy in w_copies:
        copy.wait()
    half = TOK // 2
    lo, hi = pl.ds(0, half), pl.ds(half, half)
    pass_up = remote(ag.at[1, lo], ag.at[2, lo], zs_sem.at[2], zr_sem.at[2], z_up)
    pass_down = remote(ag.at[3, hi], ag.at[2, hi], zs_sem.at[3], zr_sem.at[3], z_down)

    sends = []
    locals_ = []
    for r in (0, 1, 3, 2):
        if r == 1:
            send_up.wait_recv()
            pass_up.start()
            send_down.wait_recv()
            pass_down.start()
        if r == 2:
            pass_up.wait_recv()
            pass_down.wait_recv()
        keep_out = pltpu.make_async_copy(ag.at[r], norm_out.at[r], out_sem.at[r])
        keep_out.start()
        locals_.append(keep_out)
        for t in range(3):
            block = dot(ag[r], win[:, t * WIN : (t + 1) * WIN])
            if t == 0:
                block = block * Q_SCALE
            pt[t * WIN : (t + 1) * WIN, :] = jnp.transpose(block)
        band = lax.rem(z - r + NZ, NZ) * NX + x
        for d in (1, 3, 2, 0):
            head = lax.rem(x + d, NX)
            rows = []
            for t in range(3):
                first = pl.multiple_of(t * WIN + 32 * z + HD * head, 8)
                rows.append(pt[pl.ds(first, HD), :])
            rows.append(jnp.zeros((PACK - 3 * HD, TOK), F32))
            sendbuf[r, d] = jnp.concatenate(rows, axis=0).astype(BF16)
            if d == 0:
                copy = pltpu.make_async_copy(sendbuf.at[r, 0], qkv_out.at[band], own_sem.at[r])
                locals_.append(copy)
            else:
                copy = remote(
                    sendbuf.at[r, d], qkv_out.at[band], xs_sem.at[r, d], xr_sem.at[r, d], at(z, x + d)
                )
                sends.append(copy)
            copy.start()

    for r in (0, 1, 3, 2):
        for d in range(1, NX):
            band = lax.rem(z - r + NZ, NZ) * NX + lax.rem(x - d + NX, NX)
            remote(
                sendbuf.at[r, d], qkv_out.at[band], xs_sem.at[r, d], xr_sem.at[r, d], at(z, x + d)
            ).wait_recv()
    for copy in sends:
        copy.wait_send()
    for copy in (halo_up, halo_down, send_up, send_down, pass_up, pass_down):
        copy.wait_send()
    for copy in locals_:
        copy.wait()


def attend_kernel(
    groups,
    datas,
    qkv,
    cot,
    unit,
    inv,
    gain,
    norm_hbm,
    w_hbm,
    att,
    hgrad,
    wgrad,
    w_all,
    nall,
    p_all,
    s_ref,
    q_t,
    k_t,
    v_t,
    q_r,
    k_r,
    v_r,
    do_t,
    dos_t,
    dos_r,
    rt,
    dq,
    send_kv,
    send_q,
    recv_kv,
    recv_q,
    g_t,
    g_all,
    gw,
    send_w,
    recv_w,
    w_sem,
    nl_sem,
    ns_sem,
    nr_sem,
    kvs_sem,
    kvr_sem,
    qs_sem,
    qr_sem,
    ws_sem,
    wr_sem,
):
    me = lax.axis_index("seq")
    z = me // NX
    x = lax.rem(me, NX)
    seqs = NX * NZ
    reps = groups * datas
    mine = lax.axis_index("grp") * datas + lax.axis_index("dp")

    def rep_at(i):
        return {"grp": i // datas, "dp": lax.rem(i, datas)}

    barrier = pltpu.get_barrier_semaphore()

    def greet_seq(i, c):
        peer = {"seq": lax.rem(me + i, seqs)}
        pl.semaphore_signal(barrier, inc=1, device_id=peer, device_id_type=MESH)
        return c

    def greet_rep(i, c):
        peer = rep_at(lax.rem(mine + i, reps))
        pl.semaphore_signal(barrier, inc=1, device_id=peer, device_id_type=MESH)
        return c

    lax.fori_loop(1, seqs, greet_seq, 0)
    lax.fori_loop(1, reps, greet_rep, 0)
    w_copy = pltpu.make_async_copy(w_hbm, w_all, w_sem)
    w_copy.start()
    own_norm = pltpu.make_async_copy(norm_hbm, nall.at[0], nl_sem)
    own_norm.start()
    pl.semaphore_wait(barrier, seqs - 1 + reps - 1)

    x_up = {"seq": z * NX + lax.rem(x + 1, NX)}
    x_down = {"seq": z * NX + lax.rem(x + NX - 1, NX)}
    fst, snd = pl.ds(0, 2), pl.ds(2, 2)
    gathers = [
        remote(norm_hbm.at[fst], nall.at[1, fst], ns_sem.at[0], nr_sem.at[0], x_up),
        remote(norm_hbm.at[snd], nall.at[3, snd], ns_sem.at[1], nr_sem.at[1], x_down),
        remote(norm_hbm.at[snd], nall.at[1, snd], ns_sem.at[2], nr_sem.at[2], x_up),
        remote(norm_hbm.at[fst], nall.at[3, fst], ns_sem.at[3], nr_sem.at[3], x_down),
    ]
    relays = [
        remote(nall.at[1, fst], nall.at[2, fst], ns_sem.at[4], nr_sem.at[4], x_up),
        remote(nall.at[3, snd], nall.at[2, snd], ns_sem.at[5], nr_sem.at[5], x_down),
    ]
    for copy in gathers:
        copy.start()

    for j in range(ROWS):
        cols = slice(j * TOK, (j + 1) * TOK)
        block = qkv[j].astype(F32)
        q, k, v = block[0:HD], block[HD : 2 * HD], block[2 * HD : 3 * HD]
        q_t[:, cols] = q.astype(BF16)
        k_t[:, cols] = k.astype(BF16)
        ones = jnp.where(lax.broadcasted_iota(jnp.int32, (8, TOK), 0) == 0, 1.0, 0.0)
        v_t[:, cols] = jnp.concatenate([v, ones], axis=0).astype(BF16)
        q_r[cols, :] = jnp.transpose(q).astype(BF16)
        k_r[cols, :] = jnp.transpose(k).astype(BF16)
        v_r[cols, :] = jnp.transpose(v).astype(BF16)
        do_t[:, cols] = jnp.transpose(cot[:, j].reshape(TOK, HD).astype(F32))
    dq[...] = jnp.zeros(dq.shape, F32)

    def forward(i, c):
        cols = pl.ds(pl.multiple_of(i * QB, QB), QB)
        queries = q_t[:, cols]
        top = None
        for n in range(NQ):
            keys = slice(n * QB, (n + 1) * QB)
            s = dot(k_r[keys, :], queries)
            s_ref[keys, :] = s
            high = jnp.max(s.reshape(QB // 8, 8, QB), axis=0)
            top = high if top is None else jnp.maximum(top, high)
        top = jnp.max(top, axis=0, keepdims=True)
        out = jnp.zeros((HD + 8, QB), F32)
        for n in range(NQ):
            keys = slice(n * QB, (n + 1) * QB)
            p = jnp.exp2(s_ref[keys, :] - top).astype(BF16)
            p_all[i, keys, :] = p
            out = out + dot(v_t[:, keys], p)
        scale = 1.0 / out[HD : HD + 1, :]
        out = out[0:HD] * scale
        upstream = do_t[:, cols]
        rt[i] = jnp.broadcast_to(jnp.sum(upstream * out, axis=0, keepdims=True) * scale, (8, QB))
        upstream = upstream * scale
        dos_t[:, cols] = upstream.astype(BF16)
        dos_r[cols, :] = jnp.transpose(upstream).astype(BF16)
        out = jnp.transpose(out).astype(BF16)
        att[:, pl.ds(2 * i, 1)] = out[0:TOK].reshape(VIEWS, 1, COLS, HD)
        att[:, pl.ds(2 * i + 1, 1)] = out[TOK : 2 * TOK].reshape(VIEWS, 1, COLS, HD)
        return c

    lax.fori_loop(0, NQ, forward, 0)

    def kv_copy(band):
        return remote(
            send_kv.at[band], recv_kv.at[me], kvs_sem.at[band], kvr_sem.at[me], {"seq": band}
        )

    def q_copy(band):
        return remote(send_q.at[band], recv_q.at[me], qs_sem.at[band], qr_sem.at[me], {"seq": band})

    def backward(i, c):
        j = lax.rem(i + me // 2, NQ)
        keys = pl.ds(pl.multiple_of(j * QB, QB), QB)
        values = v_r[keys, :]
        keys_t = k_t[:, keys]
        dk = jnp.zeros((QB, HD), F32)
        dv = jnp.zeros((QB, HD), F32)
        for n in range(NQ):
            cols = slice(n * QB, (n + 1) * QB)
            p = p_all[n, keys, :]
            dp = dot(values, dos_t[:, cols])
            ds = (p.astype(F32) * (dp - rt[n][0:1])).astype(BF16)
            dv = dv + dot(p, dos_r[cols, :])
            dk = dk + dot(ds, q_r[cols, :])
            dq[:, cols] += dot(keys_t, ds)
        dk = jnp.transpose(dk * math.log(2.0))
        dv = jnp.transpose(dv)
        both = jnp.concatenate([dk, dv], axis=0).astype(BF16)
        for b in range(2):
            band = 2 * j + b
            send_kv[band] = both[:, b * TOK : (b + 1) * TOK]

            @pl.when(band != me)
            def _():
                kv_copy(band).start()

        @pl.when(i == 3)
        def _():
            gathers[0].wait_recv()
            relays[0].start()
            gathers[1].wait_recv()
            relays[1].start()

        return c

    lax.fori_loop(0, NQ, backward, 0)

    for j in range(ROWS):
        block = dq[:, j * TOK : (j + 1) * TOK] * (HD**-0.5)
        send_q[j] = jnp.concatenate([block, jnp.zeros((8, TOK), F32)], axis=0).astype(BF16)

    def start_q(i, c):
        q_copy(lax.rem(me + i, seqs)).start()
        return c

    lax.fori_loop(1, seqs, start_q, 0)
    recv_kv[me] = send_kv[me]
    recv_q[me] = send_q[me]

    own_norm.wait()
    gathers[2].wait_recv()
    gathers[3].wait_recv()
    relays[0].wait_recv()
    relays[1].wait_recv()
    for d in range(NX):
        for r in range(NZ):
            band = lax.rem(z - r + NZ, NZ) * NX + lax.rem(x - d + NX, NX)
            cols = slice((d * NZ + r) * TOK, (d * NZ + r + 1) * TOK)
            g_t[0:80, cols] = send_q[band]
            g_t[80:PACK, cols] = send_kv[band]
    for n in range(3):
        lanes = slice(n * WIN, (n + 1) * WIN)
        acc = jnp.zeros((PACK, WIN), F32)
        for d in range(NX):
            acc = acc + dot(
                g_t[:, d * 512 : (d + 1) * 512], nall[d, :, :, lanes].reshape(NZ * TOK, WIN)
            )
        acc = jnp.concatenate([acc[0:HD], acc[80:PACK], jnp.zeros((40, WIN), F32)], axis=0)
        gw[lanes, :] = jnp.transpose(acc)
    for b in range(reps):
        block = gw[b * HD : (b + 1) * HD, :]
        send_w[b] = jnp.concatenate([block, jnp.zeros((8, 256), F32)], axis=0).astype(BF16)

    def w_copy_to(i):
        return remote(send_w.at[i], recv_w.at[mine], ws_sem.at[i], wr_sem.at[mine], rep_at(i))

    def start_w(i, c):
        w_copy_to(lax.rem(mine + i, reps)).start()
        return c

    lax.fori_loop(1, reps, start_w, 0)
    recv_w[mine] = send_w[mine]

    def wait_kv(i, c):
        other = lax.rem(me + i, seqs)
        remote(
            send_kv.at[other], recv_kv.at[other], kvs_sem.at[other], kvr_sem.at[other], {"seq": other}
        ).wait_recv()
        return c

    def wait_q(i, c):
        other = lax.rem(me + i, seqs)
        remote(
            send_q.at[other], recv_q.at[other], qs_sem.at[other], qr_sem.at[other], {"seq": other}
        ).wait_recv()
        return c

    lax.fori_loop(1, seqs, wait_kv, 0)
    for h in range(0, ROWS, 2):
        one, two = recv_kv[h].astype(F32), recv_kv[h + 1].astype(F32)
        pair = jnp.concatenate([one[0:HD], two[0:HD]], axis=0)
        g_all[D + h * HD : D + (h + 2) * HD, :] = pair.astype(BF16)
        pair = jnp.concatenate([one[HD : 2 * HD], two[HD : 2 * HD]], axis=0)
        g_all[2 * D + h * HD : 2 * D + (h + 2) * HD, :] = pair.astype(BF16)
    w_copy.wait()
    normed_grad = dot(w_all[:, D : 3 * D], g_all[D : 3 * D, :])
    lax.fori_loop(1, seqs, wait_q, 0)
    for h in range(0, ROWS, 2):
        one, two = recv_q[h].astype(F32), recv_q[h + 1].astype(F32)
        pair = jnp.concatenate([one[0:HD], two[0:HD]], axis=0)
        g_all[h * HD : (h + 2) * HD, :] = pair.astype(BF16)
    normed_grad = normed_grad + dot(w_all[:, 0:D], g_all[0:D, :])
    scaled = jnp.transpose(normed_grad) * gain[...]
    u = unit[...]
    first = jnp.mean(scaled, -1, keepdims=True)
    second = jnp.mean(scaled * u, -1, keepdims=True)
    hgrad[...] = (inv[:, 0:1] * (scaled - first - u * second)).astype(BF16)

    def wait_w(i, c):
        other = lax.rem(mine + i, reps)
        remote(
            send_w.at[other], recv_w.at[other], ws_sem.at[other], wr_sem.at[other], rep_at(other)
        ).wait_recv()
        return c

    lax.fori_loop(1, reps, wait_w, 0)
    total = recv_w[0].astype(F32)
    for b in range(1, reps):
        total = total + recv_w[b].astype(F32)
    wgrad[...] = total[0:HD, 0 : 3 * HD]

    for copy in gathers + relays:
        copy.wait_send()

    def drain(i, c):
        other = lax.rem(me + i, seqs)
        kv_copy(other).wait_send()
        q_copy(other).wait_send()
        return c

    def drain_w(i, c):
        w_copy_to(lax.rem(mine + i, reps)).wait_send()
        return c

    lax.fori_loop(1, seqs, drain, 0)
    lax.fori_loop(1, reps, drain_w, 0)


VM = pl.BlockSpec(memory_space=pltpu.VMEM)
SM = pl.BlockSpec(memory_space=pltpu.SMEM)
ANY = pl.BlockSpec(memory_space=pl.ANY)
DMA = pltpu.SemaphoreType.DMA


def on_device(
    features,
    conv_weight,
    conv_bias,
    noise,
    timestep,
    camera,
    view_table,
    latent_proj,
    hidden,
    ln_gain,
    qkv_weight,
    cotangent,
):
    groups = lax.axis_size("grp")
    datas = lax.axis_size("dp")
    reps = groups * datas
    w72 = jnp.pad(conv_weight.transpose(0, 1, 3, 2), ((0, 0), (0, 0), (0, 4), (0, 0)))
    gain = ln_gain.reshape(1, D)
    qkv, norm4, unit, inv = pl.pallas_call(
        project_kernel,
        out_shape=(
            jax.ShapeDtypeStruct((ROWS, PACK, TOK), BF16),
            jax.ShapeDtypeStruct((NZ, TOK, D), BF16),
            jax.ShapeDtypeStruct((TOK, D), F32),
            jax.ShapeDtypeStruct((TOK, 128), F32),
        ),
        in_specs=[SM, SM, SM, VM, VM, VM, VM, VM, VM, VM, ANY],
        out_specs=(ANY, ANY, VM, VM),
        scratch_shapes=[
            pltpu.VMEM((2, 8, TOK), F32),
            pltpu.VMEM((2, 8, TOK), F32),
            pltpu.VMEM((NZ, TOK, D), BF16),
            pltpu.VMEM((D, 3 * WIN), BF16),
            pltpu.VMEM((3 * WIN, TOK), F32),
            pltpu.VMEM((NZ, NX, PACK, TOK), BF16),
            DMA((3,)),
            DMA((NZ,)),
            DMA((2,)),
            DMA((2,)),
            DMA((4,)),
            DMA((4,)),
            DMA((NZ, NX)),
            DMA((NZ, NX)),
            DMA((NZ,)),
        ],
        compiler_params=pltpu.CompilerParams(
            collective_id=0, has_side_effects=True, vmem_limit_bytes=40 * 2**20
        ),
        name="project",
    )(
        timestep,
        camera.reshape(VIEWS),
        conv_bias,
        features.reshape(TOK, -1),
        w72.reshape(72, -1),
        noise.reshape(TOK, 4),
        view_table,
        latent_proj,
        hidden.reshape(TOK, D),
        gain,
        qkv_weight,
    )
    att, hgrad, wgrad = pl.pallas_call(
        functools.partial(attend_kernel, groups, datas),
        out_shape=(
            jax.ShapeDtypeStruct((VIEWS, ROWS, COLS, HD), BF16),
            jax.ShapeDtypeStruct((TOK, D), BF16),
            jax.ShapeDtypeStruct((D // reps, 3 * HD), F32),
        ),
        in_specs=[VM, VM, VM, VM, VM, ANY, ANY],
        out_specs=(VM, VM, VM),
        scratch_shapes=[
            pltpu.VMEM((D, 3 * D), BF16),
            pltpu.VMEM((NX, NZ, TOK, D), BF16),
            pltpu.VMEM((NQ, 2048, QB), BF16),
            pltpu.VMEM((2048, QB), F32),
            pltpu.VMEM((HD, 2048), BF16),
            pltpu.VMEM((HD, 2048), BF16),
            pltpu.VMEM((HD + 8, 2048), BF16),
            pltpu.VMEM((2048, HD), BF16),
            pltpu.VMEM((2048, HD), BF16),
            pltpu.VMEM((2048, HD), BF16),
            pltpu.VMEM((HD, 2048), F32),
            pltpu.VMEM((HD, 2048), BF16),
            pltpu.VMEM((2048, HD), BF16),
            pltpu.VMEM((NQ, 8, QB), F32),
            pltpu.VMEM((HD, 2048), F32),
            pltpu.VMEM((ROWS, 2 * HD, TOK), BF16),
            pltpu.VMEM((ROWS, HD + 8, TOK), BF16),
            pltpu.VMEM((ROWS, 2 * HD, TOK), BF16),
            pltpu.VMEM((ROWS, HD + 8, TOK), BF16),
            pltpu.VMEM((PACK, 2048), BF16),
            pltpu.VMEM((3 * D, TOK), BF16),
            pltpu.VMEM((D, 256), F32),
            pltpu.VMEM((reps, HD + 8, 256), BF16),
            pltpu.VMEM((reps, HD + 8, 256), BF16),
            DMA,
            DMA,
            DMA((6,)),
            DMA((6,)),
            DMA((ROWS,)),
            DMA((ROWS,)),
            DMA((ROWS,)),
            DMA((ROWS,)),
            DMA((reps,)),
            DMA((reps,)),
        ],
        compiler_params=pltpu.CompilerParams(
            collective_id=1, has_side_effects=True, vmem_limit_bytes=60 * 2**20
        ),
        name="attend",
    )(qkv, cotangent.reshape(VIEWS, ROWS, COLS, HD), unit, inv, gain, norm4, qkv_weight)
    return (
        att.reshape(cotangent.shape),
        hgrad.reshape(hidden.shape),
        wgrad.reshape(1, D // reps, 3 * HD),
    )


def solution(mesh):
    return jax.shard_map(
        on_device,
        mesh=mesh,
        in_specs=(
            P(("grp", "dp"), None, "seq", None, None),
            P(),
            P(),
            P(("grp", "dp"), None, "seq", None, None),
            P(("grp", "dp")),
            P(("grp", "dp"), None),
            P(),
            P(),
            P(("grp", "dp"), None, "seq", None, None),
            P(),
            P(),
            P(("grp", "dp"), None, None, None, "seq"),
        ),
        out_specs=(
            P(("grp", "dp"), None, None, None, "seq"),
            P(("grp", "dp"), None, "seq", None, None),
            P("seq", ("grp", "dp"), None),
        ),
        check_vma=False,
    )
```

```python
import functools
import math

import jax
import jax.numpy as jnp
from jax import lax
from jax.experimental import pallas as pl
from jax.experimental.pallas import tpu as pltpu
from jax.sharding import PartitionSpec as P

MESH = pl.DeviceIdType.MESH
F32 = jnp.float32
BF16 = jnp.bfloat16
TOK = 128
VIEWS = 8
COLS = 16
ROWS = 16
D = 1152
HD = 72
NX = 4
NZ = 4
PACK = 224
WIN = 384
SEQS = NX * NZ
Q_SCALE = math.log2(math.e) / math.sqrt(HD)
QB = 256
NQ = 8


def dot(a, b):
    return jnp.dot(a, b, preferred_element_type=F32)


def remote(src, dst, send, recv, device):
    return pltpu.make_async_remote_copy(
        src_ref=src,
        dst_ref=dst,
        send_sem=send,
        recv_sem=recv,
        device_id=device,
        device_id_type=MESH,
    )


def layer_kernel(
    groups,
    datas,
    feat_h,
    w_tap_h,
    bias_h,
    noise_h,
    tstep_h,
    cam_h,
    table_h,
    latp_h,
    hid_h,
    gain_h,
    w_hbm,
    cot_h,
    att_h,
    hgrad_h,
    wgrad_h,
    feat,
    w_tap,
    noise,
    table,
    latp,
    hid,
    gain,
    cot,
    tstep,
    cam,
    bias,
    in_sem,
    halo_send,
    halo_recv,
    unit_s,
    inv_s,
    pt,
    sendbuf,
    qkv,
    w_all,
    nall,
    p_all,
    s_ref,
    q_t,
    k_t,
    v_t,
    q_r,
    k_r,
    v_r,
    do_t,
    dos_t,
    dos_r,
    rt,
    dq,
    send_kv,
    send_q,
    recv_kv,
    recv_q,
    g_t,
    g_all,
    gw,
    send_w,
    recv_w,
    att,
    hgrad,
    wgrad,
    out_sem,
    hs_sem,
    hr_sem,
    zs_sem,
    zr_sem,
    xs_sem,
    xr_sem,
    ns_sem,
    nr_sem,
    kvs_sem,
    kvr_sem,
    qs_sem,
    qr_sem,
    ws_sem,
    wr_sem,
):
    me = lax.axis_index("seq")
    z = me // NX
    x = lax.rem(me, NX)
    reps = groups * datas
    mine = lax.axis_index("grp") * datas + lax.axis_index("dp")

    def at(zz, xx):
        return {"seq": lax.rem(zz + NZ, NZ) * NX + lax.rem(xx + NX, NX)}

    def rep_at(i):
        return {"grp": i // datas, "dp": lax.rem(i, datas)}

    def band_of(d, r):
        return lax.rem(z - r + NZ, NZ) * NX + lax.rem(x - d + NX, NX)

    barrier = pltpu.get_barrier_semaphore()

    def greet_seq(i, c):
        peer = {"seq": lax.rem(me + i, SEQS)}
        pl.semaphore_signal(barrier, inc=1, device_id=peer, device_id_type=MESH)
        return c

    def greet_rep(i, c):
        peer = rep_at(lax.rem(mine + i, reps))
        pl.semaphore_signal(barrier, inc=1, device_id=peer, device_id_type=MESH)
        return c

    fetches = []
    pairs = (
        (feat_h, feat),
        (w_tap_h, w_tap),
        (noise_h, noise),
        (tstep_h, tstep),
        (cam_h, cam),
        (bias_h, bias),
        (table_h, table),
        (latp_h, latp),
        (hid_h, hid),
        (gain_h, gain),
        (w_hbm, w_all),
        (cot_h, cot),
    )
    for n, (src, dst) in enumerate(pairs):
        copy = pltpu.make_async_copy(src, dst, in_sem.at[n])
        copy.start()
        fetches.append(copy)
    lax.fori_loop(1, SEQS, greet_seq, 0)
    lax.fori_loop(1, reps, greet_rep, 0)

    fetches[0].wait()
    fetches[1].wait()
    f = feat[...].astype(F32)
    act = (f / (1.0 + jnp.exp(-f))).astype(BF16)
    lane = lax.rem(lax.broadcasted_iota(jnp.int32, (4, TOK), 1), COLS)
    part = []
    for r in range(3):
        taps = [
            lax.dot_general(
                w_tap[r * 3 + c], act, (((1,), (1,)), ((), ())), preferred_element_type=F32
            )
            for c in range(3)
        ]
        left = jnp.where(lane == 0, 0.0, pltpu.roll(taps[0], 1, 1))
        right = jnp.where(lane == COLS - 1, 0.0, pltpu.roll(taps[2], TOK - 1, 1))
        part.append(taps[1] + left + right)
    halo_send[0, 0:4] = part[0]
    halo_send[1, 0:4] = part[2]
    pl.semaphore_wait(barrier, SEQS - 1 + reps - 1)
    up = {"seq": lax.rem(me + 1, SEQS)}
    down = {"seq": lax.rem(me + SEQS - 1, SEQS)}
    halo_up = remote(halo_send.at[0], halo_recv.at[0], hs_sem.at[0], hr_sem.at[0], up)
    halo_down = remote(halo_send.at[1], halo_recv.at[1], hs_sem.at[1], hr_sem.at[1], down)
    halo_up.start()
    halo_down.start()

    for n in range(2, 10):
        fetches[n].wait()
    node = lax.broadcasted_iota(jnp.int32, (VIEWS, 64), 1)
    view = lax.broadcasted_iota(jnp.int32, (VIEWS, 64), 0)
    picked = jnp.zeros((VIEWS, 64), jnp.int32)
    for v in range(VIEWS):
        picked = jnp.where(view == v, cam[0, v], picked)
    onehot = jnp.where(node == picked, 1.0, 0.0).astype(BF16)
    embed = dot(onehot, table[...])
    base = hid[...].astype(F32).reshape(VIEWS, COLS, D) + embed[:, None, :]
    base = base.reshape(TOK, D)
    level = jnp.full((4, TOK), tstep[0], jnp.int32).astype(F32) / 1000.0
    cosine = jnp.cos((level + 0.008) / 1.008 * (math.pi / 2.0))
    signal = cosine * cosine
    keep = jnp.sqrt(signal)
    fade = jnp.sqrt(1.0 - signal)
    noises = noise[...].astype(F32)
    noises = jnp.concatenate([noises[v] for v in range(VIEWS)], axis=1)
    row = lax.broadcasted_iota(jnp.int32, (4, TOK), 0)
    bias_rows = jnp.zeros((4, TOK), F32)
    for c in range(4):
        bias_rows = jnp.where(row == c, bias[c], bias_rows)
    own = part[1] + bias_rows
    halo_up.wait_recv()
    halo_down.wait_recv()
    own = own + jnp.where(me > 0, halo_recv[0, 0:4], 0.0)
    own = own + jnp.where(me < SEQS - 1, halo_recv[1, 0:4], 0.0)
    noisy = own * keep + noises * fade
    noisy = jnp.transpose(jnp.concatenate([noisy, jnp.zeros((4, TOK), F32)], axis=0))
    inputs = base
    for c in range(4):
        inputs = inputs + noisy[:, c : c + 1] * latp[c : c + 1, :].astype(F32)

    mean = jnp.mean(inputs, -1, keepdims=True)
    centered = inputs - mean
    variance = jnp.mean(centered * centered, -1, keepdims=True)
    inverse = lax.rsqrt(variance + 1e-06)
    unit = centered * inverse
    gains = gain[...].reshape(1, D)
    nall[0, 0] = (unit * gains).astype(BF16)

    half = TOK // 2
    lo, hi = pl.ds(0, half), pl.ds(half, half)
    z_up, z_down = at(z + 1, x), at(z - 1, x)
    x_up, x_down = at(z, x + 1), at(z, x - 1)

    def gather_z(d, n):
        return (
            remote(nall.at[d, 0], nall.at[d, 1], zs_sem.at[n], zr_sem.at[n], z_up),
            remote(nall.at[d, 0], nall.at[d, 3], zs_sem.at[n + 1], zr_sem.at[n + 1], z_down),
            remote(nall.at[d, 1, lo], nall.at[d, 2, lo], zs_sem.at[n + 2], zr_sem.at[n + 2], z_up),
            remote(
                nall.at[d, 3, hi], nall.at[d, 2, hi], zs_sem.at[n + 3], zr_sem.at[n + 3], z_down
            ),
        )

    near = gather_z(0, 0)
    far = gather_z(2, 4)

    def gather_x(r):
        return (
            remote(nall.at[0, r], nall.at[1, r], ns_sem.at[r, 1], nr_sem.at[r, 1], x_up),
            remote(nall.at[0, r], nall.at[3, r], ns_sem.at[r, 3], nr_sem.at[r, 3], x_down),
        )

    side = [gather_x(r) for r in range(NZ)]
    across = remote(nall.at[0, 0], nall.at[2, 0], ns_sem.at[0, 2], nr_sem.at[0, 2], at(z, x + 2))
    near[0].start()
    near[1].start()
    unit_s[...] = unit
    inv_s[...] = jnp.broadcast_to(inverse, (TOK, 128))

    ones = jnp.where(lax.broadcasted_iota(jnp.int32, (8, TOK), 0) == 0, 1.0, 0.0)
    qkv_sends = {}

    def project(r):
        for t in range(3):
            start = pl.multiple_of(t * D + z * 256, 128)
            block = dot(nall[0, r], w_all[:, pl.ds(start, WIN)])
            if t == 0:
                block = block * Q_SCALE
            pt[t * WIN : (t + 1) * WIN, :] = jnp.transpose(block)
        for d in (1, 3, 2, 0):
            head = lax.rem(x + d, NX)
            rows = []
            for t in range(3):
                first = pl.multiple_of(t * WIN + 32 * z + HD * head, 8)
                rows.append(pt[pl.ds(first, HD), :])
            rows.append(jnp.zeros((PACK - 3 * HD, TOK), F32))
            block = jnp.concatenate(rows, axis=0).astype(BF16)
            if d == 0:
                qkv[0, r] = block
            else:
                sendbuf[r, d] = block
                copy = remote(
                    sendbuf.at[r, d], qkv.at[d, r], xs_sem.at[r, d], xr_sem.at[r, d], at(z, x + d)
                )
                copy.start()
                qkv_sends[r, d] = copy

    def spread(r):
        for d in range(NX):
            if d > 0:
                qkv_sends[r, d].wait_recv()
            n = d * NZ + r
            cols = slice(n * TOK, (n + 1) * TOK)
            block = qkv[d, r].astype(F32)
            q, k, v = block[0:HD], block[HD : 2 * HD], block[2 * HD : 3 * HD]
            q_t[:, cols] = q.astype(BF16)
            k_t[:, cols] = k.astype(BF16)
            v_t[:, cols] = jnp.concatenate([v, ones], axis=0).astype(BF16)
            q_r[cols, :] = jnp.transpose(q).astype(BF16)
            k_r[cols, :] = jnp.transpose(k).astype(BF16)
            v_r[cols, :] = jnp.transpose(v).astype(BF16)

    fetches[10].wait()
    project(0)
    side[0][0].start()
    side[0][1].start()
    across.start()
    fetches[11].wait()
    for d in range(NX):
        for r in range(NZ):
            n = d * NZ + r
            block = cot[:, pl.ds(band_of(d, r), 1)].reshape(TOK, HD).astype(F32)
            do_t[:, n * TOK : (n + 1) * TOK] = jnp.transpose(block)
    dq[...] = jnp.zeros(dq.shape, F32)
    spread(0)
    near[0].wait_recv()
    near[2].start()
    near[1].wait_recv()
    near[3].start()
    project(1)
    project(3)
    spread(1)
    spread(3)
    near[2].wait_recv()
    near[3].wait_recv()
    project(2)
    for r in (1, 3, 2):
        side[r][0].start()
        side[r][1].start()
    across.wait_recv()
    far[0].start()
    far[1].start()
    spread(2)

    def forward(i, c):
        cols = pl.ds(pl.multiple_of(i * QB, QB), QB)
        queries = q_t[:, cols]
        top = None
        for n in range(NQ):
            keys = slice(n * QB, (n + 1) * QB)
            s = dot(k_r[keys, :], queries)
            s_ref[keys, :] = s
            high = jnp.max(s.reshape(QB // 8, 8, QB), axis=0)
            top = high if top is None else jnp.maximum(top, high)
        top = jnp.max(top, axis=0, keepdims=True)
        out = jnp.zeros((HD + 8, QB), F32)
        for n in range(NQ):
            keys = slice(n * QB, (n + 1) * QB)
            p = jnp.exp2(s_ref[keys, :] - top).astype(BF16)
            p_all[i, keys, :] = p
            out = out + dot(v_t[:, keys], p)
        scale = 1.0 / out[HD : HD + 1, :]
        out = out[0:HD] * scale
        upstream = do_t[:, cols]
        rt[i] = jnp.broadcast_to(jnp.sum(upstream * out, axis=0, keepdims=True) * scale, (8, QB))
        upstream = upstream * scale
        dos_t[:, cols] = upstream.astype(BF16)
        dos_r[cols, :] = jnp.transpose(upstream).astype(BF16)
        out = jnp.transpose(out).astype(BF16)
        for b in range(2):
            band = band_of(i // 2, lax.rem(i, 2) * 2 + b)
            block = out[b * TOK : (b + 1) * TOK].reshape(VIEWS, 1, COLS, HD)
            att[:, pl.ds(band, 1)] = block
        return c

    lax.fori_loop(0, NQ, forward, 0)
    att_out = pltpu.make_async_copy(att, att_h, out_sem.at[0])
    att_out.start()

    def kv_copy(pos, band):
        return remote(
            send_kv.at[pos], recv_kv.at[me], kvs_sem.at[pos], kvr_sem.at[me], {"seq": band}
        )

    def q_copy(pos, band):
        return remote(send_q.at[pos], recv_q.at[me], qs_sem.at[pos], qr_sem.at[me], {"seq": band})

    def backward(j, c):
        keys = pl.ds(pl.multiple_of(j * QB, QB), QB)
        values = v_r[keys, :]
        keys_t = k_t[:, keys]
        dk = jnp.zeros((QB, HD), F32)
        dv = jnp.zeros((QB, HD), F32)
        for n in range(NQ):
            cols = slice(n * QB, (n + 1) * QB)
            p = p_all[n, keys, :]
            dp = dot(values, dos_t[:, cols])
            ds = (p.astype(F32) * (dp - rt[n][0:1])).astype(BF16)
            dv = dv + dot(p, dos_r[cols, :])
            dk = dk + dot(ds, q_r[cols, :])
            dq[:, cols] += dot(keys_t, ds)
        dk = jnp.transpose(dk * math.log(2.0))
        dv = jnp.transpose(dv)
        both = jnp.concatenate([dk, dv], axis=0).astype(BF16)
        for b in range(2):
            pos = 2 * j + b
            send_kv[pos] = both[:, b * TOK : (b + 1) * TOK]

            @pl.when(pos > 0)
            def _():
                kv_copy(pos, band_of(pos // NZ, lax.rem(pos, NZ))).start()

        @pl.when(j == 3)
        def _():
            far[0].wait_recv()
            far[2].start()
            far[1].wait_recv()
            far[3].start()

        return c

    lax.fori_loop(0, NQ, backward, 0)

    for pos in range(SEQS):
        block = dq[:, pos * TOK : (pos + 1) * TOK] * (HD**-0.5)
        send_q[pos] = jnp.concatenate([block, jnp.zeros((8, TOK), F32)], axis=0).astype(BF16)
        if pos > 0:
            q_copy(pos, band_of(pos // NZ, pos % NZ)).start()
    recv_kv[me] = send_kv[0]
    recv_q[me] = send_q[0]

    for pos in range(SEQS):
        cols = slice(pos * TOK, (pos + 1) * TOK)
        g_t[0:80, cols] = send_q[pos]
        g_t[80:PACK, cols] = send_kv[pos]
    for r in (1, 3, 2):
        side[r][0].wait_recv()
        side[r][1].wait_recv()
    side[0][0].wait_recv()
    side[0][1].wait_recv()
    far[2].wait_recv()
    far[3].wait_recv()
    for n in range(3):
        lanes = slice(n * WIN, (n + 1) * WIN)
        acc = jnp.zeros((PACK, WIN), F32)
        for d in range(NX):
            acc = acc + dot(
                g_t[:, d * 512 : (d + 1) * 512], nall[d, :, :, lanes].reshape(NZ * TOK, WIN)
            )
        acc = jnp.concatenate([acc[0:HD], acc[80:PACK], jnp.zeros((40, WIN), F32)], axis=0)
        gw[lanes, :] = jnp.transpose(acc)
    for b in range(reps):
        block = gw[b * HD : (b + 1) * HD, :]
        send_w[b] = jnp.concatenate([block, jnp.zeros((8, 256), F32)], axis=0).astype(BF16)

    def w_copy_to(i):
        return remote(send_w.at[i], recv_w.at[mine], ws_sem.at[i], wr_sem.at[mine], rep_at(i))

    def start_w(i, c):
        w_copy_to(lax.rem(mine + i, reps)).start()
        return c

    lax.fori_loop(1, reps, start_w, 0)
    recv_w[mine] = send_w[mine]

    def wait_kv(i, c):
        other = lax.rem(me + i, SEQS)
        remote(
            send_kv.at[0], recv_kv.at[other], kvs_sem.at[0], kvr_sem.at[other], {"seq": other}
        ).wait_recv()
        return c

    def wait_q(i, c):
        other = lax.rem(me + i, SEQS)
        remote(
            send_q.at[0], recv_q.at[other], qs_sem.at[0], qr_sem.at[other], {"seq": other}
        ).wait_recv()
        return c

    lax.fori_loop(1, SEQS, wait_kv, 0)
    for h in range(0, SEQS, 2):
        one, two = recv_kv[h].astype(F32), recv_kv[h + 1].astype(F32)
        pair = jnp.concatenate([one[0:HD], two[0:HD]], axis=0)
        g_all[D + h * HD : D + (h + 2) * HD, :] = pair.astype(BF16)
        pair = jnp.concatenate([one[HD : 2 * HD], two[HD : 2 * HD]], axis=0)
        g_all[2 * D + h * HD : 2 * D + (h + 2) * HD, :] = pair.astype(BF16)
    normed_grad = dot(w_all[:, D : 3 * D], g_all[D : 3 * D, :])
    lax.fori_loop(1, SEQS, wait_q, 0)
    for h in range(0, SEQS, 2):
        one, two = recv_q[h].astype(F32), recv_q[h + 1].astype(F32)
        pair = jnp.concatenate([one[0:HD], two[0:HD]], axis=0)
        g_all[h * HD : (h + 2) * HD, :] = pair.astype(BF16)
    normed_grad = normed_grad + dot(w_all[:, 0:D], g_all[0:D, :])
    scaled = jnp.transpose(normed_grad) * gain[...].reshape(1, D)
    u = unit_s[...]
    first = jnp.mean(scaled, -1, keepdims=True)
    second = jnp.mean(scaled * u, -1, keepdims=True)
    hgrad[...] = (inv_s[:, 0:1] * (scaled - first - u * second)).astype(BF16)
    hgrad_out = pltpu.make_async_copy(hgrad, hgrad_h, out_sem.at[1])
    hgrad_out.start()

    def wait_w(i, c):
        other = lax.rem(mine + i, reps)
        remote(
            send_w.at[0], recv_w.at[other], ws_sem.at[0], wr_sem.at[other], rep_at(other)
        ).wait_recv()
        return c

    lax.fori_loop(1, reps, wait_w, 0)
    total = recv_w[0].astype(F32)
    for b in range(1, reps):
        total = total + recv_w[b].astype(F32)
    wgrad[...] = total[0:HD, 0 : 3 * HD]
    wgrad_out = pltpu.make_async_copy(wgrad, wgrad_h, out_sem.at[2])
    wgrad_out.start()

    for copy in (halo_up, halo_down, across) + near + far:
        copy.wait_send()
    for pair in side:
        pair[0].wait_send()
        pair[1].wait_send()
    for copy in qkv_sends.values():
        copy.wait_send()

    def drain(i, c):
        kv_copy(i, lax.rem(me + i, SEQS)).wait_send()
        q_copy(i, lax.rem(me + i, SEQS)).wait_send()
        return c

    def drain_w(i, c):
        w_copy_to(lax.rem(mine + i, reps)).wait_send()
        return c

    lax.fori_loop(1, SEQS, drain, 0)
    lax.fori_loop(1, reps, drain_w, 0)
    att_out.wait()
    hgrad_out.wait()
    wgrad_out.wait()


def hand_out(*refs):
    count = len(refs) // 2
    sem = refs[-1]
    copies = [
        pltpu.make_async_copy(refs[n], refs[count + n], sem.at[n]) for n in range(count)
    ]
    for copy in copies:
        copy.start()
    for copy in copies:
        copy.wait()


ANY = pl.BlockSpec(memory_space=pl.ANY)
DMA = pltpu.SemaphoreType.DMA


def on_device(
    features,
    conv_weight,
    conv_bias,
    noise,
    timestep,
    camera,
    view_table,
    latent_proj,
    hidden,
    ln_gain,
    qkv_weight,
    cotangent,
):
    groups = lax.axis_size("grp")
    datas = lax.axis_size("dp")
    reps = groups * datas
    depth = features.shape[-1]
    outs = (
        jax.ShapeDtypeStruct((VIEWS, ROWS, COLS, HD), BF16),
        jax.ShapeDtypeStruct((TOK, D), BF16),
        jax.ShapeDtypeStruct((D // reps, 3 * HD), F32),
    )
    results = pl.pallas_call(
        functools.partial(layer_kernel, groups, datas),
        out_shape=outs,
        in_specs=[ANY] * 12,
        out_specs=(ANY,) * 3,
        scratch_shapes=[
            pltpu.VMEM((TOK, depth), BF16),
            pltpu.VMEM((9, 4, depth), BF16),
            pltpu.VMEM((VIEWS, 4, COLS), BF16),
            pltpu.VMEM(view_table.shape, BF16),
            pltpu.VMEM(latent_proj.shape, BF16),
            pltpu.VMEM((TOK, D), BF16),
            pltpu.VMEM((D,), F32),
            pltpu.VMEM((VIEWS, ROWS, COLS, HD), BF16),
            pltpu.SMEM((1,), jnp.int32),
            pltpu.SMEM((1, VIEWS), jnp.int32),
            pltpu.SMEM((4,), F32),
            DMA((12,)),
            pltpu.VMEM((2, 8, TOK), F32),
            pltpu.VMEM((2, 8, TOK), F32),
            pltpu.VMEM((TOK, D), F32),
            pltpu.VMEM((TOK, 128), F32),
            pltpu.VMEM((3 * WIN, TOK), F32),
            pltpu.VMEM((NZ, NX, PACK, TOK), BF16),
            pltpu.VMEM((NX, NZ, PACK, TOK), BF16),
            pltpu.VMEM((D, 3 * D), BF16),
            pltpu.VMEM((NX, NZ, TOK, D), BF16),
            pltpu.VMEM((NQ, 2048, QB), BF16),
            pltpu.VMEM((2048, QB), F32),
            pltpu.VMEM((HD, 2048), BF16),
            pltpu.VMEM((HD, 2048), BF16),
            pltpu.VMEM((HD + 8, 2048), BF16),
            pltpu.VMEM((2048, HD), BF16),
            pltpu.VMEM((2048, HD), BF16),
            pltpu.VMEM((2048, HD), BF16),
            pltpu.VMEM((HD, 2048), F32),
            pltpu.VMEM((HD, 2048), BF16),
            pltpu.VMEM((2048, HD), BF16),
            pltpu.VMEM((NQ, 8, QB), F32),
            pltpu.VMEM((HD, 2048), F32),
            pltpu.VMEM((SEQS, 2 * HD, TOK), BF16),
            pltpu.VMEM((SEQS, HD + 8, TOK), BF16),
            pltpu.VMEM((SEQS, 2 * HD, TOK), BF16),
            pltpu.VMEM((SEQS, HD + 8, TOK), BF16),
            pltpu.VMEM((PACK, 2048), BF16),
            pltpu.VMEM((3 * D, TOK), BF16),
            pltpu.VMEM((D, 256), F32),
            pltpu.VMEM((reps, HD + 8, 256), BF16),
            pltpu.VMEM((reps, HD + 8, 256), BF16),
            pltpu.VMEM((VIEWS, ROWS, COLS, HD), BF16),
            pltpu.VMEM((TOK, D), BF16),
            pltpu.VMEM((D // reps, 3 * HD), F32),
            DMA((3,)),
            DMA((2,)),
            DMA((2,)),
            DMA((8,)),
            DMA((8,)),
            DMA((NZ, NX)),
            DMA((NZ, NX)),
            DMA((NZ, NX)),
            DMA((NZ, NX)),
            DMA((SEQS,)),
            DMA((SEQS,)),
            DMA((SEQS,)),
            DMA((SEQS,)),
            DMA((reps,)),
            DMA((reps,)),
        ],
        compiler_params=pltpu.CompilerParams(
            collective_id=0, has_side_effects=True, vmem_limit_bytes=62 * 2**20
        ),
        name="layer",
    )(
        features.reshape(TOK, depth),
        conv_weight.transpose(0, 1, 3, 2).reshape(9, 4, depth),
        conv_bias,
        noise.transpose(0, 1, 2, 4, 3).reshape(VIEWS, 4, COLS),
        timestep,
        camera,
        view_table,
        latent_proj,
        hidden.reshape(TOK, D),
        ln_gain,
        qkv_weight,
        cotangent.reshape(VIEWS, ROWS, COLS, HD),
    )
    att, hgrad, wgrad = pl.pallas_call(
        hand_out,
        out_shape=outs,
        in_specs=[ANY] * 3,
        out_specs=(ANY,) * 3,
        scratch_shapes=[DMA((3,))],
        name="hand_out",
    )(*results)
    return (
        att.reshape(cotangent.shape),
        hgrad.reshape(hidden.shape),
        wgrad.reshape(1, D // reps, 3 * HD),
    )


def solution(mesh):
    return jax.shard_map(
        on_device,
        mesh=mesh,
        in_specs=(
            P(("grp", "dp"), None, "seq", None, None),
            P(),
            P(),
            P(("grp", "dp"), None, "seq", None, None),
            P(("grp", "dp")),
            P(("grp", "dp"), None),
            P(),
            P(),
            P(("grp", "dp"), None, "seq", None, None),
            P(),
            P(),
            P(("grp", "dp"), None, None, None, "seq"),
        ),
        out_specs=(
            P(("grp", "dp"), None, None, None, "seq"),
            P(("grp", "dp"), None, "seq", None, None),
            P("seq", ("grp", "dp"), None),
        ),
        check_vma=False,
    )
```

```python
import functools
import math

import jax
import jax.numpy as jnp
from jax import lax
from jax.experimental import pallas as pl
from jax.experimental.pallas import tpu as pltpu
from jax.sharding import PartitionSpec as P

MESH = pl.DeviceIdType.MESH
F32 = jnp.float32
BF16 = jnp.bfloat16
TOK = 128
VIEWS = 8
COLS = 16
ROWS = 16
D = 1152
HD = 72
NX = 4
NZ = 4
PACK = 224
WIN = 384
SEQS = NX * NZ
Q_SCALE = math.log2(math.e) / math.sqrt(HD)
QB = 256
NQ = 8
GROUP = 512
ORDER = (0, 1, 3, 2)


def dot(a, b):
    return jnp.dot(a, b, preferred_element_type=F32)


def remote(src, dst, send, recv, device):
    return pltpu.make_async_remote_copy(
        src_ref=src,
        dst_ref=dst,
        send_sem=send,
        recv_sem=recv,
        device_id=device,
        device_id_type=MESH,
    )


def layer_kernel(
    groups,
    datas,
    feat_h,
    w_tap_h,
    bias_h,
    noise_h,
    tstep_h,
    cam_h,
    table_h,
    latp_h,
    hid_h,
    gain_h,
    w_hbm,
    cot_h,
    att_h,
    hgrad_h,
    wgrad_h,
    feat,
    w_tap,
    noise,
    table,
    latp,
    hid,
    gain,
    cot,
    tstep,
    cam,
    bias,
    in_sem,
    halo_send,
    halo_recv,
    unit_s,
    inv_s,
    pt,
    sendbuf,
    qkv,
    w_all,
    nall,
    p_all,
    s_all,
    tops,
    q_t,
    k_t,
    v_t,
    q_r,
    k_r,
    v_r,
    do_t,
    dos_t,
    dos_r,
    rt,
    dq,
    ds_s,
    send_kv,
    send_q,
    recv_kv,
    recv_q,
    g_t,
    g_all,
    gw,
    send_p,
    recv_p,
    send_w,
    recv_w,
    att,
    hgrad,
    wgrad,
    out_sem,
    hs_sem,
    hr_sem,
    zs_sem,
    zr_sem,
    xs_sem,
    xr_sem,
    ns_sem,
    nr_sem,
    rs_sem,
    rr_sem,
    kvs_sem,
    kvr_sem,
    qs_sem,
    qr_sem,
    ps_sem,
    pr_sem,
    ws_sem,
    wr_sem,
):
    me = lax.axis_index("seq")
    z = me // NX
    x = lax.rem(me, NX)
    chips = groups * datas // 2
    dp = lax.axis_index("dp")
    core = lax.rem(dp, 2)
    chip = lax.axis_index("grp") * (datas // 2) + dp // 2
    partner = {"dp": dp + 1 - 2 * core}

    def at(zz, xx):
        return {"seq": lax.rem(zz + NZ, NZ) * NX + lax.rem(xx + NX, NX)}

    def chip_at(k):
        return {"grp": k // (datas // 2), "dp": lax.rem(k, datas // 2) * 2 + core}

    def band_of(d, r):
        return lax.rem(z - r + NZ, NZ) * NX + lax.rem(x - d + NX, NX)

    barrier = pltpu.get_barrier_semaphore()

    def greet_seq(i, c):
        peer = {"seq": lax.rem(me + i, SEQS)}
        pl.semaphore_signal(barrier, inc=1, device_id=peer, device_id_type=MESH)
        return c

    def greet_chip(i, c):
        peer = chip_at(lax.rem(chip + i, chips))
        pl.semaphore_signal(barrier, inc=1, device_id=peer, device_id_type=MESH)
        return c

    fetches = []
    pairs = (
        (feat_h, feat),
        (w_tap_h, w_tap),
        (noise_h, noise),
        (tstep_h, tstep),
        (cam_h, cam),
        (bias_h, bias),
        (table_h, table),
        (latp_h, latp),
        (hid_h, hid),
        (gain_h, gain),
        (w_hbm, w_all),
        (cot_h, cot),
    )
    for n, (src, dst) in enumerate(pairs):
        copy = pltpu.make_async_copy(src, dst, in_sem.at[n])
        copy.start()
        fetches.append(copy)
    lax.fori_loop(1, SEQS, greet_seq, 0)
    lax.fori_loop(1, chips, greet_chip, 0)
    pl.semaphore_signal(barrier, inc=1, device_id=partner, device_id_type=MESH)

    fetches[0].wait()
    fetches[1].wait()
    f = feat[...].astype(F32)
    act = (f / (1.0 + jnp.exp(-f))).astype(BF16)
    lane = lax.rem(lax.broadcasted_iota(jnp.int32, (4, TOK), 1), COLS)
    part = []
    for r in range(3):
        taps = [
            lax.dot_general(
                w_tap[r * 3 + c], act, (((1,), (1,)), ((), ())), preferred_element_type=F32
            )
            for c in range(3)
        ]
        left = jnp.where(lane == 0, 0.0, pltpu.roll(taps[0], 1, 1))
        right = jnp.where(lane == COLS - 1, 0.0, pltpu.roll(taps[2], TOK - 1, 1))
        part.append(taps[1] + left + right)
    halo_send[0, 0:4] = part[0]
    halo_send[1, 0:4] = part[2]
    pl.semaphore_wait(barrier, SEQS - 1 + chips)
    up = {"seq": lax.rem(me + 1, SEQS)}
    down = {"seq": lax.rem(me + SEQS - 1, SEQS)}
    halo_up = remote(halo_send.at[0], halo_recv.at[0], hs_sem.at[0], hr_sem.at[0], up)
    halo_down = remote(halo_send.at[1], halo_recv.at[1], hs_sem.at[1], hr_sem.at[1], down)
    halo_up.start()
    halo_down.start()

    for n in range(2, 10):
        fetches[n].wait()
    node = lax.broadcasted_iota(jnp.int32, (VIEWS, 64), 1)
    view = lax.broadcasted_iota(jnp.int32, (VIEWS, 64), 0)
    picked = jnp.zeros((VIEWS, 64), jnp.int32)
    for v in range(VIEWS):
        picked = jnp.where(view == v, cam[0, v], picked)
    onehot = jnp.where(node == picked, 1.0, 0.0).astype(BF16)
    embed = dot(onehot, table[...])
    base = hid[...].astype(F32).reshape(VIEWS, COLS, D) + embed[:, None, :]
    base = base.reshape(TOK, D)
    level = jnp.full((4, TOK), tstep[0], jnp.int32).astype(F32) / 1000.0
    cosine = jnp.cos((level + 0.008) / 1.008 * (math.pi / 2.0))
    signal = cosine * cosine
    keep = jnp.sqrt(signal)
    fade = jnp.sqrt(1.0 - signal)
    noises = noise[...].astype(F32)
    noises = jnp.concatenate([noises[v] for v in range(VIEWS)], axis=1)
    row = lax.broadcasted_iota(jnp.int32, (4, TOK), 0)
    bias_rows = jnp.zeros((4, TOK), F32)
    for c in range(4):
        bias_rows = jnp.where(row == c, bias[c], bias_rows)
    own = part[1] + bias_rows
    halo_up.wait_recv()
    halo_down.wait_recv()
    own = own + jnp.where(me > 0, halo_recv[0, 0:4], 0.0)
    own = own + jnp.where(me < SEQS - 1, halo_recv[1, 0:4], 0.0)
    noisy = own * keep + noises * fade
    noisy = jnp.transpose(jnp.concatenate([noisy, jnp.zeros((4, TOK), F32)], axis=0))
    inputs = base
    for c in range(4):
        inputs = inputs + noisy[:, c : c + 1] * latp[c : c + 1, :].astype(F32)

    mean = jnp.mean(inputs, -1, keepdims=True)
    centered = inputs - mean
    variance = jnp.mean(centered * centered, -1, keepdims=True)
    inverse = lax.rsqrt(variance + 1e-06)
    unit = centered * inverse
    gains = gain[...].reshape(1, D)
    nall[0, 0] = (unit * gains).astype(BF16)

    half = TOK // 2
    lo, hi = pl.ds(0, half), pl.ds(half, half)
    z_up, z_down = at(z + 1, x), at(z - 1, x)
    x_up, x_down, x_far = at(z, x + 1), at(z, x - 1), at(z, x + 2)

    def by_z(src, dst, n, device):
        return remote(src, dst, zs_sem.at[n], zr_sem.at[n], device)

    up_lo = by_z(nall.at[0, 0, lo], nall.at[1, 0, lo], 0, z_up)
    up_hi = by_z(nall.at[0, 0, hi], nall.at[1, 0, hi], 1, z_up)
    down_hi = by_z(nall.at[0, 0, hi], nall.at[2, 0, hi], 2, z_down)
    down_lo = by_z(nall.at[0, 0, lo], nall.at[2, 0, lo], 3, z_down)
    pass_lo = by_z(nall.at[1, 0, lo], nall.at[3, 0, lo], 4, z_up)
    pass_hi = by_z(nall.at[2, 0, hi], nall.at[3, 0, hi], 5, z_down)
    far_up = by_z(nall.at[0, 2], nall.at[1, 2], 6, z_up)
    far_down = by_z(nall.at[0, 2], nall.at[2, 2], 7, z_down)

    def by_x(n, d, device):
        return remote(nall.at[n, 0], nall.at[n, d], ns_sem.at[n, d], nr_sem.at[n, d], device)

    side = [(by_x(n, 1, x_up), by_x(n, 3, x_down)) for n in range(NZ)]
    relays = []
    for n in (0, 3):
        relay = n // 3 * 2
        relays.append(
            (
                remote(
                    nall.at[n, 1, lo], nall.at[n, 2, lo], rs_sem.at[relay], rr_sem.at[relay], x_up
                ),
                remote(
                    nall.at[n, 3, hi],
                    nall.at[n, 2, hi],
                    rs_sem.at[relay + 1],
                    rr_sem.at[relay + 1],
                    x_down,
                ),
            )
        )

    def relay_x(n):
        for k in range(2):
            side[n * 3][k].wait_recv()
            relays[n][k].start()

    for copy in (up_lo, down_hi, up_hi, down_lo):
        copy.start()
    unit_s[...] = unit
    inv_s[...] = jnp.broadcast_to(inverse, (TOK, 128))

    ones = jnp.where(lax.broadcasted_iota(jnp.int32, (8, TOK), 0) == 0, 1.0, 0.0)
    qkv_sends = {}

    def project(n):
        for t in range(3):
            start = pl.multiple_of(t * D + z * 256, 128)
            block = dot(nall[n, 0], w_all[:, pl.ds(start, WIN)])
            if t == 0:
                block = block * Q_SCALE
            pt[t * WIN : (t + 1) * WIN, :] = jnp.transpose(block)
        for d in (2, 1, 3, 0):
            head = lax.rem(x + d, NX)
            rows = []
            for t in range(3):
                first = pl.multiple_of(t * WIN + 32 * z + HD * head, 8)
                rows.append(pt[pl.ds(first, HD), :])
            rows.append(jnp.zeros((PACK - 3 * HD, TOK), F32))
            block = jnp.concatenate(rows, axis=0).astype(BF16)
            if d == 0:
                qkv[n, 0] = block
            else:
                sendbuf[n, d] = block
                copy = remote(
                    sendbuf.at[n, d], qkv.at[n, d], xs_sem.at[n, d], xr_sem.at[n, d], at(z, x + d)
                )
                copy.start()
                qkv_sends[n, d] = copy

    def spread(n):
        for d in range(NX):
            if d > 0:
                qkv_sends[n, d].wait_recv()
            pos = n * NX + d
            cols = slice(pos * TOK, (pos + 1) * TOK)
            block = qkv[n, d].astype(F32)
            q, k, v = block[0:HD], block[HD : 2 * HD], block[2 * HD : 3 * HD]
            q_t[:, cols] = q.astype(BF16)
            k_t[:, cols] = k.astype(BF16)
            v_t[:, cols] = jnp.concatenate([v, ones], axis=0).astype(BF16)
            q_r[cols, :] = jnp.transpose(q).astype(BF16)
            k_r[cols, :] = jnp.transpose(k).astype(BF16)
            v_r[cols, :] = jnp.transpose(v).astype(BF16)

    def score(group, first, last):
        cols = slice(group * GROUP, (group + 1) * GROUP)
        queries = q_t[:, cols]
        top = None
        for n in range(first, last):
            keys = slice(n * QB, (n + 1) * QB)
            s = dot(k_r[keys, :], queries)
            s_all[keys, cols] = s
            high = jnp.max(s.reshape(QB // 8, 8, GROUP), axis=0)
            top = high if top is None else jnp.maximum(top, high)
        return top

    fetches[10].wait()
    project(0)
    for copy in side[0]:
        copy.start()
    fetches[11].wait()
    for n in range(NZ):
        for d in range(NX):
            pos = n * NX + d
            block = cot[:, pl.ds(band_of(d, ORDER[n]), 1)].reshape(TOK, HD).astype(F32)
            do_t[:, pos * TOK : (pos + 1) * TOK] = jnp.transpose(block)
    dq[...] = jnp.zeros(dq.shape, F32)
    up_lo.wait_recv()
    pass_lo.start()
    down_hi.wait_recv()
    pass_hi.start()
    spread(0)
    relay_x(0)
    up_hi.wait_recv()
    project(1)
    down_lo.wait_recv()
    project(2)
    side[1][0].start()
    side[1][1].start()
    spread(1)
    spread(2)
    pass_lo.wait_recv()
    pass_hi.wait_recv()
    project(3)
    for n in (3, 2):
        side[n][0].start()
        side[n][1].start()
    for copy in relays[0]:
        copy.wait_recv()
    far_up.start()
    far_down.start()

    for group in range(NZ - 1):
        tops[group] = score(group, 0, 6)
    spread(3)
    for group in range(NZ - 1):
        tops[group] = jnp.maximum(tops[group], score(group, 6, NQ))
    tops[3] = score(3, 0, NQ)
    for group in range(NZ):
        cols = slice(group * GROUP, (group + 1) * GROUP)
        top = jnp.max(tops[group], axis=0, keepdims=True)
        out = None
        for n in range(NQ):
            keys = slice(n * QB, (n + 1) * QB)
            p = jnp.exp2(s_all[keys, cols] - top).astype(BF16)
            p_all[keys, cols] = p
            term = dot(v_t[:, keys], p)
            out = term if out is None else out + term
        scale = 1.0 / out[HD : HD + 1, :]
        out = out[0:HD] * scale
        upstream = do_t[:, cols]
        total = jnp.sum(upstream * out, axis=0, keepdims=True) * scale
        rt[:, cols] = jnp.broadcast_to(total, (8, GROUP))
        upstream = upstream * scale
        dos_t[:, cols] = upstream.astype(BF16)
        dos_r[cols, :] = jnp.transpose(upstream).astype(BF16)
        out = jnp.transpose(out).astype(BF16)
        for d in range(NX):
            block = out[d * TOK : (d + 1) * TOK].reshape(VIEWS, 1, COLS, HD)
            att[:, pl.ds(band_of(d, ORDER[group]), 1)] = block
    att_out = pltpu.make_async_copy(att, att_h, out_sem.at[0])
    att_out.start()

    def kv_copy(pos, band):
        return remote(
            send_kv.at[pos], recv_kv.at[me], kvs_sem.at[pos], kvr_sem.at[me], {"seq": band}
        )

    def q_copy(pos, band):
        return remote(send_q.at[pos], recv_q.at[me], qs_sem.at[pos], qr_sem.at[me], {"seq": band})

    def score_grad(keys):
        values = v_r[keys, :]
        for n in range(NQ):
            cols = slice(n * QB, (n + 1) * QB)
            dp = dot(values, dos_t[:, cols])
            p = p_all[keys, cols].astype(F32)
            ds_s[:, cols] = (p * (dp - rt[0:1, cols])).astype(BF16)

    def key_grads(keys):
        dv = dot(p_all[keys, :], dos_r[...])
        dk = dot(ds_s[...], q_r[...])
        dk = jnp.transpose(dk * math.log(2.0))
        dv = jnp.transpose(dv)
        both = jnp.concatenate([dk, dv], axis=0).astype(BF16)
        g_t[80:PACK, keys] = both
        return both

    def backward(i, c):
        n = NZ - 1 - i
        keys = pl.ds(pl.multiple_of(n * GROUP, GROUP), GROUP)
        score_grad(keys)
        dq[...] += dot(k_t[:, keys], ds_s[...])
        both = key_grads(keys)
        row = jnp.where(n == 1, 1, 5 - n)
        for d in range(NX):
            pos = n * NX + d
            send_kv[pos] = both[:, d * TOK : (d + 1) * TOK]
            kv_copy(pos, band_of(d, row)).start()
        return c

    lax.fori_loop(0, 1, backward, 0)
    relay_x(1)
    lax.fori_loop(1, NZ - 1, backward, 0)
    keys = slice(0, GROUP)
    score_grad(keys)
    for n in range(NZ - 1, -1, -1):
        cols = slice(n * GROUP, (n + 1) * GROUP)
        block = (dq[:, cols] + dot(k_t[:, keys], ds_s[:, cols])) * (HD**-0.5)
        block = jnp.concatenate([block, jnp.zeros((8, GROUP), F32)], axis=0).astype(BF16)
        g_t[0:80, cols] = block
        for d in range(NX):
            pos = n * NX + d
            send_q[pos] = block[:, d * TOK : (d + 1) * TOK]
            if pos > 0:
                q_copy(pos, band_of(d, ORDER[n])).start()
    both = key_grads(keys)
    for d in range(NX):
        send_kv[d] = both[:, d * TOK : (d + 1) * TOK]
        if d > 0:
            kv_copy(d, band_of(d, 0)).start()
    recv_kv[me] = send_kv[0]
    recv_q[me] = send_q[0]

    for n in (1, 2):
        side[n][0].wait_recv()
        side[n][1].wait_recv()
    far_up.wait_recv()
    far_down.wait_recv()
    for copy in relays[1]:
        copy.wait_recv()
    for n in range(3):
        lanes = slice(n * WIN, (n + 1) * WIN)
        acc = dot(g_t[...], nall[:, :, :, lanes].reshape(SEQS * TOK, WIN))
        acc = jnp.concatenate([acc[0:HD], acc[80:PACK], jnp.zeros((40, WIN), F32)], axis=0)
        gw[lanes, :] = jnp.transpose(acc)

    def w_rows(b):
        return pl.ds(pl.multiple_of(b * HD, 8), HD)

    spare = jnp.zeros((8, 256), F32)
    for k in range(chips):
        block = gw[w_rows(2 * k + 1 - core), :]
        send_p[k] = jnp.concatenate([block, spare], axis=0).astype(BF16)
    pair_copy = remote(send_p, recv_p, ps_sem, pr_sem, partner)
    pair_copy.start()

    def wait_kv(i, c):
        other = lax.rem(me + i, SEQS)
        remote(
            send_kv.at[0], recv_kv.at[other], kvs_sem.at[0], kvr_sem.at[other], {"seq": other}
        ).wait_recv()
        return c

    def wait_q(i, c):
        other = lax.rem(me + i, SEQS)
        remote(
            send_q.at[0], recv_q.at[other], qs_sem.at[0], qr_sem.at[other], {"seq": other}
        ).wait_recv()
        return c

    lax.fori_loop(1, SEQS, wait_kv, 0)
    for h in range(0, SEQS, 2):
        one, two = recv_kv[h].astype(F32), recv_kv[h + 1].astype(F32)
        pair = jnp.concatenate([one[0:HD], two[0:HD]], axis=0)
        g_all[D + h * HD : D + (h + 2) * HD, :] = pair.astype(BF16)
        pair = jnp.concatenate([one[HD : 2 * HD], two[HD : 2 * HD]], axis=0)
        g_all[2 * D + h * HD : 2 * D + (h + 2) * HD, :] = pair.astype(BF16)

    def w_copy_to(k):
        return remote(send_w.at[k], recv_w.at[chip], ws_sem.at[k], wr_sem.at[chip], chip_at(k))

    pair_copy.wait_recv()
    for k in range(chips):
        block = gw[w_rows(2 * k + core), :] + recv_p[k].astype(F32)[0:HD]
        send_w[k] = jnp.concatenate([block, spare], axis=0).astype(BF16)

    def start_w(i, c):
        w_copy_to(lax.rem(chip + i, chips)).start()
        return c

    lax.fori_loop(1, chips, start_w, 0)
    recv_w[chip] = send_w[chip]

    normed_grad = dot(w_all[:, D : 3 * D], g_all[D : 3 * D, :])
    lax.fori_loop(1, SEQS, wait_q, 0)
    for h in range(0, SEQS, 2):
        one, two = recv_q[h].astype(F32), recv_q[h + 1].astype(F32)
        pair = jnp.concatenate([one[0:HD], two[0:HD]], axis=0)
        g_all[h * HD : (h + 2) * HD, :] = pair.astype(BF16)
    normed_grad = normed_grad + dot(w_all[:, 0:D], g_all[0:D, :])
    scaled = jnp.transpose(normed_grad) * gain[...].reshape(1, D)
    u = unit_s[...]
    first = jnp.mean(scaled, -1, keepdims=True)
    second = jnp.mean(scaled * u, -1, keepdims=True)
    hgrad[...] = (inv_s[:, 0:1] * (scaled - first - u * second)).astype(BF16)
    hgrad_out = pltpu.make_async_copy(hgrad, hgrad_h, out_sem.at[1])
    hgrad_out.start()

    def wait_w(i, c):
        other = lax.rem(chip + i, chips)
        remote(
            send_w.at[0], recv_w.at[other], ws_sem.at[0], wr_sem.at[other], chip_at(other)
        ).wait_recv()
        return c

    lax.fori_loop(1, chips, wait_w, 0)
    total = recv_w[0].astype(F32)
    for k in range(1, chips):
        total = total + recv_w[k].astype(F32)
    wgrad[...] = total[0:HD, 0 : 3 * HD]
    wgrad_out = pltpu.make_async_copy(wgrad, wgrad_h, out_sem.at[2])
    wgrad_out.start()

    zs = (up_lo, up_hi, down_hi, down_lo, pass_lo, pass_hi, far_up, far_down)
    for copy in (halo_up, halo_down, pair_copy) + zs + relays[0] + relays[1]:
        copy.wait_send()
    for pair in side:
        pair[0].wait_send()
        pair[1].wait_send()
    for copy in qkv_sends.values():
        copy.wait_send()

    def drain(i, c):
        kv_copy(i, lax.rem(me + i, SEQS)).wait_send()
        q_copy(i, lax.rem(me + i, SEQS)).wait_send()
        return c

    def drain_w(i, c):
        w_copy_to(lax.rem(chip + i, chips)).wait_send()
        return c

    lax.fori_loop(1, SEQS, drain, 0)
    lax.fori_loop(1, chips, drain_w, 0)
    att_out.wait()
    hgrad_out.wait()
    wgrad_out.wait()


def hand_out(*refs):
    count = len(refs) // 2
    sem = refs[-1]
    copies = [
        pltpu.make_async_copy(refs[n], refs[count + n], sem.at[n]) for n in range(count)
    ]
    for copy in copies:
        copy.start()
    for copy in copies:
        copy.wait()


ANY = pl.BlockSpec(memory_space=pl.ANY)
DMA = pltpu.SemaphoreType.DMA


def on_device(
    features,
    conv_weight,
    conv_bias,
    noise,
    timestep,
    camera,
    view_table,
    latent_proj,
    hidden,
    ln_gain,
    qkv_weight,
    cotangent,
):
    groups = lax.axis_size("grp")
    datas = lax.axis_size("dp")
    reps = groups * datas
    depth = features.shape[-1]
    outs = (
        jax.ShapeDtypeStruct((VIEWS, ROWS, COLS, HD), BF16),
        jax.ShapeDtypeStruct((TOK, D), BF16),
        jax.ShapeDtypeStruct((D // reps, 3 * HD), F32),
    )
    results = pl.pallas_call(
        functools.partial(layer_kernel, groups, datas),
        out_shape=outs,
        in_specs=[ANY] * 12,
        out_specs=(ANY,) * 3,
        scratch_shapes=[
            pltpu.VMEM((TOK, depth), BF16),
            pltpu.VMEM((9, 4, depth), BF16),
            pltpu.VMEM((VIEWS, 4, COLS), BF16),
            pltpu.VMEM(view_table.shape, BF16),
            pltpu.VMEM(latent_proj.shape, BF16),
            pltpu.VMEM((TOK, D), BF16),
            pltpu.VMEM((D,), F32),
            pltpu.VMEM((VIEWS, ROWS, COLS, HD), BF16),
            pltpu.SMEM((1,), jnp.int32),
            pltpu.SMEM((1, VIEWS), jnp.int32),
            pltpu.SMEM((4,), F32),
            DMA((12,)),
            pltpu.VMEM((2, 8, TOK), F32),
            pltpu.VMEM((2, 8, TOK), F32),
            pltpu.VMEM((TOK, D), F32),
            pltpu.VMEM((TOK, 128), F32),
            pltpu.VMEM((3 * WIN, TOK), F32),
            pltpu.VMEM((NZ, NX, PACK, TOK), BF16),
            pltpu.VMEM((NX, NZ, PACK, TOK), BF16),
            pltpu.VMEM((D, 3 * D), BF16),
            pltpu.VMEM((NX, NZ, TOK, D), BF16),
            pltpu.VMEM((2048, 2048), BF16),
            pltpu.VMEM((2048, 2048), F32),
            pltpu.VMEM((NZ, 8, GROUP), F32),
            pltpu.VMEM((HD, 2048), BF16),
            pltpu.VMEM((HD, 2048), BF16),
            pltpu.VMEM((HD + 8, 2048), BF16),
            pltpu.VMEM((2048, HD), BF16),
            pltpu.VMEM((2048, HD), BF16),
            pltpu.VMEM((2048, HD), BF16),
            pltpu.VMEM((HD, 2048), F32),
            pltpu.VMEM((HD, 2048), BF16),
            pltpu.VMEM((2048, HD), BF16),
            pltpu.VMEM((8, 2048), F32),
            pltpu.VMEM((HD, 2048), F32),
            pltpu.VMEM((GROUP, 2048), BF16),
            pltpu.VMEM((SEQS, 2 * HD, TOK), BF16),
            pltpu.VMEM((SEQS, HD + 8, TOK), BF16),
            pltpu.VMEM((SEQS, 2 * HD, TOK), BF16),
            pltpu.VMEM((SEQS, HD + 8, TOK), BF16),
            pltpu.VMEM((PACK, 2048), BF16),
            pltpu.VMEM((3 * D, TOK), BF16),
            pltpu.VMEM((D, 256), F32),
            pltpu.VMEM((reps // 2, HD + 8, 256), BF16),
            pltpu.VMEM((reps // 2, HD + 8, 256), BF16),
            pltpu.VMEM((reps // 2, HD + 8, 256), BF16),
            pltpu.VMEM((reps // 2, HD + 8, 256), BF16),
            pltpu.VMEM((VIEWS, ROWS, COLS, HD), BF16),
            pltpu.VMEM((TOK, D), BF16),
            pltpu.VMEM((D // reps, 3 * HD), F32),
            DMA((3,)),
            DMA((2,)),
            DMA((2,)),
            DMA((8,)),
            DMA((8,)),
            DMA((NZ, NX)),
            DMA((NZ, NX)),
            DMA((NZ, NX)),
            DMA((NZ, NX)),
            DMA((4,)),
            DMA((4,)),
            DMA((SEQS,)),
            DMA((SEQS,)),
            DMA((SEQS,)),
            DMA((SEQS,)),
            DMA,
            DMA,
            DMA((reps // 2,)),
            DMA((reps // 2,)),
        ],
        compiler_params=pltpu.CompilerParams(
            collective_id=0, has_side_effects=True, vmem_limit_bytes=62 * 2**20
        ),
        name="layer",
    )(
        features.reshape(TOK, depth),
        conv_weight.transpose(0, 1, 3, 2).reshape(9, 4, depth),
        conv_bias,
        noise.transpose(0, 1, 2, 4, 3).reshape(VIEWS, 4, COLS),
        timestep,
        camera,
        view_table,
        latent_proj,
        hidden.reshape(TOK, D),
        ln_gain,
        qkv_weight,
        cotangent.reshape(VIEWS, ROWS, COLS, HD),
    )
    att, hgrad, wgrad = pl.pallas_call(
        hand_out,
        out_shape=outs,
        in_specs=[ANY] * 3,
        out_specs=(pl.BlockSpec(memory_space=pltpu.VMEM),) * 3,
        scratch_shapes=[DMA((3,))],
        compiler_params=pltpu.CompilerParams(vmem_limit_bytes=62 * 2**20),
        name="hand_out",
    )(*results)
    return (
        att.reshape(cotangent.shape),
        hgrad.reshape(hidden.shape),
        wgrad.reshape(1, D // reps, 3 * HD),
    )


def solution(mesh):
    return jax.shard_map(
        on_device,
        mesh=mesh,
        in_specs=(
            P(("grp", "dp"), None, "seq", None, None),
            P(),
            P(),
            P(("grp", "dp"), None, "seq", None, None),
            P(("grp", "dp")),
            P(("grp", "dp"), None),
            P(),
            P(),
            P(("grp", "dp"), None, "seq", None, None),
            P(),
            P(),
            P(("grp", "dp"), None, None, None, "seq"),
        ),
        out_specs=(
            P(("grp", "dp"), None, None, None, "seq"),
            P(("grp", "dp"), None, "seq", None, None),
            P("seq", ("grp", "dp"), None),
        ),
        check_vma=False,
    )
```

```python
import functools
import math

import jax
import jax.numpy as jnp
from jax import lax
from jax.experimental import pallas as pl
from jax.experimental.pallas import tpu as pltpu
from jax.sharding import PartitionSpec as P

MESH = pl.DeviceIdType.MESH
F32 = jnp.float32
BF16 = jnp.bfloat16
TOK = 128
VIEWS = 8
COLS = 16
ROWS = 16
D = 1152
HD = 72
NX = 4
NZ = 4
PACK = 224
WIN = 384
SEQS = NX * NZ
Q_SCALE = math.log2(math.e) / math.sqrt(HD)
QB = 256
NQ = 8
GROUP = 512
ORDER = (0, 1, 3, 2)


def dot(a, b):
    return jnp.dot(a, b, preferred_element_type=F32)


def remote(src, dst, send, recv, device):
    return pltpu.make_async_remote_copy(
        src_ref=src,
        dst_ref=dst,
        send_sem=send,
        recv_sem=recv,
        device_id=device,
        device_id_type=MESH,
    )


def layer_kernel(
    groups,
    datas,
    feat_h,
    w_tap_h,
    bias_h,
    noise_h,
    tstep_h,
    cam_h,
    table_h,
    latp_h,
    hid_h,
    gain_h,
    w_hbm,
    cot_h,
    att_h,
    hgrad_h,
    wgrad_h,
    feat,
    w_tap,
    noise,
    table,
    latp,
    hid,
    gain,
    cot,
    tstep,
    cam,
    bias,
    in_sem,
    halo_send,
    halo_recv,
    unit_s,
    inv_s,
    pt,
    sendbuf,
    qkv,
    w_all,
    nall,
    p_all,
    s_all,
    tops,
    q_t,
    k_t,
    v_t,
    q_r,
    k_r,
    v_r,
    do_t,
    dos_t,
    dos_r,
    rt,
    dq,
    ds_s,
    send_kv,
    send_q,
    recv_kv,
    recv_q,
    g_t,
    g_all,
    gw,
    send_p,
    recv_p,
    send_w,
    recv_w,
    att,
    hgrad,
    wgrad,
    out_sem,
    hs_sem,
    hr_sem,
    zs_sem,
    zr_sem,
    xs_sem,
    xr_sem,
    ns_sem,
    nr_sem,
    rs_sem,
    rr_sem,
    kvs_sem,
    kvr_sem,
    qs_sem,
    qr_sem,
    ps_sem,
    pr_sem,
    ws_sem,
    wr_sem,
):
    me = lax.axis_index("seq")
    z = me // NX
    x = lax.rem(me, NX)
    chips = groups * datas // 2
    dp = lax.axis_index("dp")
    core = lax.rem(dp, 2)
    chip = lax.axis_index("grp") * (datas // 2) + dp // 2
    partner = {"dp": dp + 1 - 2 * core}

    def at(zz, xx):
        return {"seq": lax.rem(zz + NZ, NZ) * NX + lax.rem(xx + NX, NX)}

    def chip_at(k):
        return {"grp": k // (datas // 2), "dp": lax.rem(k, datas // 2) * 2 + core}

    def band_of(d, r):
        return lax.rem(z - r + NZ, NZ) * NX + lax.rem(x - d + NX, NX)

    barrier = pltpu.get_barrier_semaphore()

    def greet_seq(i, c):
        peer = {"seq": lax.rem(me + i, SEQS)}
        pl.semaphore_signal(barrier, inc=1, device_id=peer, device_id_type=MESH)
        return c

    def greet_chip(i, c):
        peer = chip_at(lax.rem(chip + i, chips))
        pl.semaphore_signal(barrier, inc=1, device_id=peer, device_id_type=MESH)
        return c

    fetches = []
    pairs = (
        (feat_h, feat),
        (w_tap_h, w_tap),
        (noise_h, noise),
        (tstep_h, tstep),
        (cam_h, cam),
        (bias_h, bias),
        (table_h, table),
        (latp_h, latp),
        (hid_h, hid),
        (gain_h, gain),
        (w_hbm, w_all),
        (cot_h, cot),
    )
    for n, (src, dst) in enumerate(pairs):
        copy = pltpu.make_async_copy(src, dst, in_sem.at[n])
        copy.start()
        fetches.append(copy)
    lax.fori_loop(1, SEQS, greet_seq, 0)
    lax.fori_loop(1, chips, greet_chip, 0)
    pl.semaphore_signal(barrier, inc=1, device_id=partner, device_id_type=MESH)

    fetches[0].wait()
    fetches[1].wait()
    f = feat[...].astype(F32)
    act = (f / (1.0 + jnp.exp(-f))).astype(BF16)
    lane = lax.rem(lax.broadcasted_iota(jnp.int32, (4, TOK), 1), COLS)
    part = []
    for r in range(3):
        taps = [
            lax.dot_general(
                w_tap[r * 3 + c], act, (((1,), (1,)), ((), ())), preferred_element_type=F32
            )
            for c in range(3)
        ]
        left = jnp.where(lane == 0, 0.0, pltpu.roll(taps[0], 1, 1))
        right = jnp.where(lane == COLS - 1, 0.0, pltpu.roll(taps[2], TOK - 1, 1))
        part.append(taps[1] + left + right)
    halo_send[0, 0:4] = part[0]
    halo_send[1, 0:4] = part[2]
    pl.semaphore_wait(barrier, SEQS - 1 + chips)
    up = {"seq": lax.rem(me + 1, SEQS)}
    down = {"seq": lax.rem(me + SEQS - 1, SEQS)}
    halo_up = remote(halo_send.at[0], halo_recv.at[0], hs_sem.at[0], hr_sem.at[0], up)
    halo_down = remote(halo_send.at[1], halo_recv.at[1], hs_sem.at[1], hr_sem.at[1], down)
    halo_up.start()
    halo_down.start()

    for n in range(2, 10):
        fetches[n].wait()
    node = lax.broadcasted_iota(jnp.int32, (VIEWS, 64), 1)
    view = lax.broadcasted_iota(jnp.int32, (VIEWS, 64), 0)
    picked = jnp.zeros((VIEWS, 64), jnp.int32)
    for v in range(VIEWS):
        picked = jnp.where(view == v, cam[0, v], picked)
    onehot = jnp.where(node == picked, 1.0, 0.0).astype(BF16)
    embed = dot(onehot, table[...])
    base = hid[...].astype(F32).reshape(VIEWS, COLS, D) + embed[:, None, :]
    base = base.reshape(TOK, D)
    level = jnp.full((4, TOK), tstep[0], jnp.int32).astype(F32) / 1000.0
    cosine = jnp.cos((level + 0.008) / 1.008 * (math.pi / 2.0))
    signal = cosine * cosine
    keep = jnp.sqrt(signal)
    fade = jnp.sqrt(1.0 - signal)
    noises = noise[...].astype(F32)
    noises = jnp.concatenate([noises[v] for v in range(VIEWS)], axis=1)
    row = lax.broadcasted_iota(jnp.int32, (4, TOK), 0)
    bias_rows = jnp.zeros((4, TOK), F32)
    for c in range(4):
        bias_rows = jnp.where(row == c, bias[c], bias_rows)
    own = part[1] + bias_rows
    halo_up.wait_recv()
    halo_down.wait_recv()
    own = own + jnp.where(me > 0, halo_recv[0, 0:4], 0.0)
    own = own + jnp.where(me < SEQS - 1, halo_recv[1, 0:4], 0.0)
    noisy = own * keep + noises * fade
    noisy = jnp.transpose(jnp.concatenate([noisy, jnp.zeros((4, TOK), F32)], axis=0))
    inputs = base
    for c in range(4):
        inputs = inputs + noisy[:, c : c + 1] * latp[c : c + 1, :].astype(F32)

    mean = jnp.mean(inputs, -1, keepdims=True)
    centered = inputs - mean
    variance = jnp.mean(centered * centered, -1, keepdims=True)
    inverse = lax.rsqrt(variance + 1e-06)
    unit = centered * inverse
    gains = gain[...].reshape(1, D)
    nall[0, 0] = (unit * gains).astype(BF16)

    half = TOK // 2
    lo, hi = pl.ds(0, half), pl.ds(half, half)
    z_up, z_down = at(z + 1, x), at(z - 1, x)
    x_up, x_down, x_far = at(z, x + 1), at(z, x - 1), at(z, x + 2)

    def by_z(src, dst, n, device):
        return remote(src, dst, zs_sem.at[n], zr_sem.at[n], device)

    up_lo = by_z(nall.at[0, 0, lo], nall.at[1, 0, lo], 0, z_up)
    up_hi = by_z(nall.at[0, 0, hi], nall.at[1, 0, hi], 1, z_up)
    down_hi = by_z(nall.at[0, 0, hi], nall.at[2, 0, hi], 2, z_down)
    down_lo = by_z(nall.at[0, 0, lo], nall.at[2, 0, lo], 3, z_down)
    pass_lo = by_z(nall.at[1, 0, lo], nall.at[3, 0, lo], 4, z_up)
    pass_hi = by_z(nall.at[2, 0, hi], nall.at[3, 0, hi], 5, z_down)
    far_up = by_z(nall.at[0, 2], nall.at[1, 2], 6, z_up)
    far_down = by_z(nall.at[0, 2], nall.at[2, 2], 7, z_down)

    def by_x(n, d, device):
        return remote(nall.at[n, 0], nall.at[n, d], ns_sem.at[n, d], nr_sem.at[n, d], device)

    side = [(by_x(n, 1, x_up), by_x(n, 3, x_down)) for n in range(NZ)]
    relays = []
    for n in (0, 3):
        relay = n // 3 * 2
        relays.append(
            (
                remote(
                    nall.at[n, 1, lo], nall.at[n, 2, lo], rs_sem.at[relay], rr_sem.at[relay], x_up
                ),
                remote(
                    nall.at[n, 3, hi],
                    nall.at[n, 2, hi],
                    rs_sem.at[relay + 1],
                    rr_sem.at[relay + 1],
                    x_down,
                ),
            )
        )

    def relay_x(n):
        for k in range(2):
            side[n * 3][k].wait_recv()
            relays[n][k].start()

    for copy in (up_lo, down_hi, up_hi, down_lo):
        copy.start()
    unit_s[...] = unit
    inv_s[...] = jnp.broadcast_to(inverse, (TOK, 128))

    ones = jnp.where(lax.broadcasted_iota(jnp.int32, (8, TOK), 0) == 0, 1.0, 0.0)
    qkv_sends = {}

    def project(n):
        for t in range(3):
            start = pl.multiple_of(t * D + z * 256, 128)
            block = dot(nall[n, 0], w_all[:, pl.ds(start, WIN)])
            if t == 0:
                block = block * Q_SCALE
            pt[t * WIN : (t + 1) * WIN, :] = jnp.transpose(block)
        for d in (2, 1, 3, 0):
            head = lax.rem(x + d, NX)
            rows = []
            for t in range(3):
                first = pl.multiple_of(t * WIN + 32 * z + HD * head, 8)
                rows.append(pt[pl.ds(first, HD), :])
            rows.append(jnp.zeros((PACK - 3 * HD, TOK), F32))
            block = jnp.concatenate(rows, axis=0).astype(BF16)
            if d == 0:
                qkv[n, 0] = block
            else:
                sendbuf[n, d] = block
                copy = remote(
                    sendbuf.at[n, d], qkv.at[n, d], xs_sem.at[n, d], xr_sem.at[n, d], at(z, x + d)
                )
                copy.start()
                qkv_sends[n, d] = copy

    def spread(n):
        for d in range(NX):
            if d > 0:
                qkv_sends[n, d].wait_recv()
            pos = n * NX + d
            cols = slice(pos * TOK, (pos + 1) * TOK)
            block = qkv[n, d].astype(F32)
            q, k, v = block[0:HD], block[HD : 2 * HD], block[2 * HD : 3 * HD]
            q_t[:, cols] = q.astype(BF16)
            k_t[:, cols] = k.astype(BF16)
            v_t[:, cols] = jnp.concatenate([v, ones], axis=0).astype(BF16)
            q_r[cols, :] = jnp.transpose(q).astype(BF16)
            k_r[cols, :] = jnp.transpose(k).astype(BF16)
            v_r[cols, :] = jnp.transpose(v).astype(BF16)

    def score(group, first, last):
        cols = slice(group * GROUP, (group + 1) * GROUP)
        queries = q_t[:, cols]
        top = None
        for n in range(first, last):
            keys = slice(n * QB, (n + 1) * QB)
            s = dot(k_r[keys, :], queries)
            s_all[keys, cols] = s
            high = jnp.max(s.reshape(QB // 8, 8, GROUP), axis=0)
            top = high if top is None else jnp.maximum(top, high)
        return top

    fetches[10].wait()
    project(0)
    for copy in side[0]:
        copy.start()
    fetches[11].wait()
    for n in range(NZ):
        for d in range(NX):
            pos = n * NX + d
            block = cot[:, pl.ds(band_of(d, ORDER[n]), 1)].reshape(TOK, HD).astype(F32)
            do_t[:, pos * TOK : (pos + 1) * TOK] = jnp.transpose(block)
    dq[...] = jnp.zeros(dq.shape, F32)
    up_lo.wait_recv()
    pass_lo.start()
    down_hi.wait_recv()
    pass_hi.start()
    spread(0)
    relay_x(0)
    up_hi.wait_recv()
    project(1)
    down_lo.wait_recv()
    project(2)
    side[1][0].start()
    side[1][1].start()
    spread(1)
    spread(2)
    pass_lo.wait_recv()
    pass_hi.wait_recv()
    project(3)
    for n in (3, 2):
        side[n][0].start()
        side[n][1].start()
    for copy in relays[0]:
        copy.wait_recv()
    far_up.start()
    far_down.start()

    for group in range(NZ - 1):
        tops[group] = score(group, 0, 6)
    spread(3)
    for group in range(NZ - 1):
        tops[group] = jnp.maximum(tops[group], score(group, 6, NQ))
    tops[3] = score(3, 0, NQ)
    for group in range(NZ):
        cols = slice(group * GROUP, (group + 1) * GROUP)
        top = jnp.max(tops[group], axis=0, keepdims=True)
        out = None
        for n in range(NQ):
            keys = slice(n * QB, (n + 1) * QB)
            p = jnp.exp2(s_all[keys, cols] - top).astype(BF16)
            p_all[keys, cols] = p
            term = dot(v_t[:, keys], p)
            out = term if out is None else out + term
        scale = 1.0 / out[HD : HD + 1, :]
        out = out[0:HD] * scale
        upstream = do_t[:, cols]
        total = jnp.sum(upstream * out, axis=0, keepdims=True) * scale
        rt[:, cols] = jnp.broadcast_to(total, (8, GROUP))
        upstream = upstream * scale
        dos_t[:, cols] = upstream.astype(BF16)
        dos_r[cols, :] = jnp.transpose(upstream).astype(BF16)
        out = jnp.transpose(out).astype(BF16)
        for d in range(NX):
            block = out[d * TOK : (d + 1) * TOK].reshape(VIEWS, 1, COLS, HD)
            att[:, pl.ds(band_of(d, ORDER[group]), 1)] = block
    att_out = pltpu.make_async_copy(att, att_h, out_sem.at[0])
    att_out.start()

    def kv_copy(pos, band):
        return remote(
            send_kv.at[pos], recv_kv.at[me], kvs_sem.at[pos], kvr_sem.at[me], {"seq": band}
        )

    def q_copy(pos, band):
        return remote(send_q.at[pos], recv_q.at[me], qs_sem.at[pos], qr_sem.at[me], {"seq": band})

    def score_grad(keys):
        values = v_r[keys, :]
        for n in range(NQ):
            cols = slice(n * QB, (n + 1) * QB)
            dp = dot(values, dos_t[:, cols])
            p = p_all[keys, cols].astype(F32)
            ds_s[:, cols] = (p * (dp - rt[0:1, cols])).astype(BF16)

    def key_grads(keys):
        dv = dot(p_all[keys, :], dos_r[...])
        dk = dot(ds_s[...], q_r[...])
        dk = jnp.transpose(dk * math.log(2.0))
        dv = jnp.transpose(dv)
        both = jnp.concatenate([dk, dv], axis=0).astype(BF16)
        g_t[80:PACK, keys] = both
        return both

    def backward(i, c):
        n = NZ - 1 - i
        keys = pl.ds(pl.multiple_of(n * GROUP, GROUP), GROUP)
        score_grad(keys)
        dq[...] += dot(k_t[:, keys], ds_s[...])
        both = key_grads(keys)
        row = jnp.where(n == 1, 1, 5 - n)
        for d in range(NX):
            pos = n * NX + d
            send_kv[pos] = both[:, d * TOK : (d + 1) * TOK]
            kv_copy(pos, band_of(d, row)).start()
        return c

    lax.fori_loop(0, 1, backward, 0)
    relay_x(1)
    lax.fori_loop(1, NZ - 1, backward, 0)
    keys = slice(0, GROUP)
    score_grad(keys)
    for n in range(NZ - 1, -1, -1):
        cols = slice(n * GROUP, (n + 1) * GROUP)
        block = (dq[:, cols] + dot(k_t[:, keys], ds_s[:, cols])) * (HD**-0.5)
        block = jnp.concatenate([block, jnp.zeros((8, GROUP), F32)], axis=0).astype(BF16)
        g_t[0:80, cols] = block
        for d in range(NX):
            pos = n * NX + d
            send_q[pos] = block[:, d * TOK : (d + 1) * TOK]
            if pos > 0:
                q_copy(pos, band_of(d, ORDER[n])).start()
    both = key_grads(keys)
    for d in range(NX):
        send_kv[d] = both[:, d * TOK : (d + 1) * TOK]
        if d > 0:
            kv_copy(d, band_of(d, 0)).start()
    recv_kv[me] = send_kv[0]
    recv_q[me] = send_q[0]

    def partial_w(first, last, lanes):
        tokens = nall[first:last, :, :, lanes].reshape((last - first) * GROUP, WIN)
        return dot(g_t[:, first * GROUP : last * GROUP], tokens)

    side[1][0].wait_recv()
    side[1][1].wait_recv()
    far_up.wait_recv()
    for n in range(3):
        lanes = slice(n * WIN, (n + 1) * WIN)
        s_all[0:PACK, lanes] = partial_w(0, 2, lanes)
    side[2][0].wait_recv()
    side[2][1].wait_recv()
    far_down.wait_recv()
    for copy in relays[1]:
        copy.wait_recv()
    for n in range(3):
        lanes = slice(n * WIN, (n + 1) * WIN)
        acc = s_all[0:PACK, lanes] + partial_w(2, 4, lanes)
        acc = jnp.concatenate([acc[0:HD], acc[80:PACK], jnp.zeros((40, WIN), F32)], axis=0)
        gw[lanes, :] = jnp.transpose(acc)

    def w_rows(b):
        return pl.ds(pl.multiple_of(b * HD, 8), HD)

    spare = jnp.zeros((8, 256), F32)
    for k in range(chips):
        block = gw[w_rows(2 * k + 1 - core), :]
        send_p[k] = jnp.concatenate([block, spare], axis=0).astype(BF16)
    pair_copy = remote(send_p, recv_p, ps_sem, pr_sem, partner)
    pair_copy.start()

    def wait_kv(i, c):
        other = lax.rem(me + i, SEQS)
        remote(
            send_kv.at[0], recv_kv.at[other], kvs_sem.at[0], kvr_sem.at[other], {"seq": other}
        ).wait_recv()
        return c

    def wait_q(i, c):
        other = lax.rem(me + i, SEQS)
        remote(
            send_q.at[0], recv_q.at[other], qs_sem.at[0], qr_sem.at[other], {"seq": other}
        ).wait_recv()
        return c

    def w_copy_to(k):
        return remote(send_w.at[k], recv_w.at[chip], ws_sem.at[k], wr_sem.at[chip], chip_at(k))

    pair_copy.wait_recv()
    for k in range(chips):
        block = gw[w_rows(2 * k + core), :] + recv_p[k].astype(F32)[0:HD]
        send_w[k] = jnp.concatenate([block, spare], axis=0).astype(BF16)

    def start_w(i, c):
        w_copy_to(lax.rem(chip + i, chips)).start()
        return c

    lax.fori_loop(1, chips, start_w, 0)
    recv_w[chip] = send_w[chip]

    lax.fori_loop(1, SEQS, wait_kv, 0)
    for h in range(0, SEQS, 2):
        one, two = recv_kv[h].astype(F32), recv_kv[h + 1].astype(F32)
        pair = jnp.concatenate([one[0:HD], two[0:HD]], axis=0)
        g_all[D + h * HD : D + (h + 2) * HD, :] = pair.astype(BF16)
        pair = jnp.concatenate([one[HD : 2 * HD], two[HD : 2 * HD]], axis=0)
        g_all[2 * D + h * HD : 2 * D + (h + 2) * HD, :] = pair.astype(BF16)

    normed_grad = dot(w_all[:, D : 3 * D], g_all[D : 3 * D, :])
    lax.fori_loop(1, SEQS, wait_q, 0)
    for h in range(0, SEQS, 2):
        one, two = recv_q[h].astype(F32), recv_q[h + 1].astype(F32)
        pair = jnp.concatenate([one[0:HD], two[0:HD]], axis=0)
        g_all[h * HD : (h + 2) * HD, :] = pair.astype(BF16)
    normed_grad = normed_grad + dot(w_all[:, 0:D], g_all[0:D, :])
    scaled = jnp.transpose(normed_grad) * gain[...].reshape(1, D)
    u = unit_s[...]
    first = jnp.mean(scaled, -1, keepdims=True)
    second = jnp.mean(scaled * u, -1, keepdims=True)
    hgrad[...] = (inv_s[:, 0:1] * (scaled - first - u * second)).astype(BF16)
    hgrad_out = pltpu.make_async_copy(hgrad, hgrad_h, out_sem.at[1])
    hgrad_out.start()

    def wait_w(i, c):
        other = lax.rem(chip + i, chips)
        remote(
            send_w.at[0], recv_w.at[other], ws_sem.at[0], wr_sem.at[other], chip_at(other)
        ).wait_recv()
        return c

    lax.fori_loop(1, chips, wait_w, 0)
    total = recv_w[0].astype(F32)
    for k in range(1, chips):
        total = total + recv_w[k].astype(F32)
    wgrad[...] = total[0:HD, 0 : 3 * HD]
    wgrad_out = pltpu.make_async_copy(wgrad, wgrad_h, out_sem.at[2])
    wgrad_out.start()

    zs = (up_lo, up_hi, down_hi, down_lo, pass_lo, pass_hi, far_up, far_down)
    for copy in (halo_up, halo_down, pair_copy) + zs + relays[0] + relays[1]:
        copy.wait_send()
    for pair in side:
        pair[0].wait_send()
        pair[1].wait_send()
    for copy in qkv_sends.values():
        copy.wait_send()

    def drain(i, c):
        kv_copy(i, lax.rem(me + i, SEQS)).wait_send()
        q_copy(i, lax.rem(me + i, SEQS)).wait_send()
        return c

    def drain_w(i, c):
        w_copy_to(lax.rem(chip + i, chips)).wait_send()
        return c

    lax.fori_loop(1, SEQS, drain, 0)
    lax.fori_loop(1, chips, drain_w, 0)
    att_out.wait()
    hgrad_out.wait()
    wgrad_out.wait()


def hand_out(*refs):
    count = len(refs) // 2
    sem = refs[-1]
    copies = [
        pltpu.make_async_copy(refs[n], refs[count + n], sem.at[n]) for n in range(count)
    ]
    for copy in copies:
        copy.start()
    for copy in copies:
        copy.wait()


ANY = pl.BlockSpec(memory_space=pl.ANY)
DMA = pltpu.SemaphoreType.DMA


def on_device(
    features,
    conv_weight,
    conv_bias,
    noise,
    timestep,
    camera,
    view_table,
    latent_proj,
    hidden,
    ln_gain,
    qkv_weight,
    cotangent,
):
    groups = lax.axis_size("grp")
    datas = lax.axis_size("dp")
    reps = groups * datas
    depth = features.shape[-1]
    outs = (
        jax.ShapeDtypeStruct((VIEWS, ROWS, COLS, HD), BF16),
        jax.ShapeDtypeStruct((TOK, D), BF16),
        jax.ShapeDtypeStruct((D // reps, 3 * HD), F32),
    )
    results = pl.pallas_call(
        functools.partial(layer_kernel, groups, datas),
        out_shape=outs,
        in_specs=[ANY] * 12,
        out_specs=(ANY,) * 3,
        scratch_shapes=[
            pltpu.VMEM((TOK, depth), BF16),
            pltpu.VMEM((9, 4, depth), BF16),
            pltpu.VMEM((VIEWS, 4, COLS), BF16),
            pltpu.VMEM(view_table.shape, BF16),
            pltpu.VMEM(latent_proj.shape, BF16),
            pltpu.VMEM((TOK, D), BF16),
            pltpu.VMEM((D,), F32),
            pltpu.VMEM((VIEWS, ROWS, COLS, HD), BF16),
            pltpu.SMEM((1,), jnp.int32),
            pltpu.SMEM((1, VIEWS), jnp.int32),
            pltpu.SMEM((4,), F32),
            DMA((12,)),
            pltpu.VMEM((2, 8, TOK), F32),
            pltpu.VMEM((2, 8, TOK), F32),
            pltpu.VMEM((TOK, D), F32),
            pltpu.VMEM((TOK, 128), F32),
            pltpu.VMEM((3 * WIN, TOK), F32),
            pltpu.VMEM((NZ, NX, PACK, TOK), BF16),
            pltpu.VMEM((NX, NZ, PACK, TOK), BF16),
            pltpu.VMEM((D, 3 * D), BF16),
            pltpu.VMEM((NX, NZ, TOK, D), BF16),
            pltpu.VMEM((2048, 2048), BF16),
            pltpu.VMEM((2048, 2048), F32),
            pltpu.VMEM((NZ, 8, GROUP), F32),
            pltpu.VMEM((HD, 2048), BF16),
            pltpu.VMEM((HD, 2048), BF16),
            pltpu.VMEM((HD + 8, 2048), BF16),
            pltpu.VMEM((2048, HD), BF16),
            pltpu.VMEM((2048, HD), BF16),
            pltpu.VMEM((2048, HD), BF16),
            pltpu.VMEM((HD, 2048), F32),
            pltpu.VMEM((HD, 2048), BF16),
            pltpu.VMEM((2048, HD), BF16),
            pltpu.VMEM((8, 2048), F32),
            pltpu.VMEM((HD, 2048), F32),
            pltpu.VMEM((GROUP, 2048), BF16),
            pltpu.VMEM((SEQS, 2 * HD, TOK), BF16),
            pltpu.VMEM((SEQS, HD + 8, TOK), BF16),
            pltpu.VMEM((SEQS, 2 * HD, TOK), BF16),
            pltpu.VMEM((SEQS, HD + 8, TOK), BF16),
            pltpu.VMEM((PACK, 2048), BF16),
            pltpu.VMEM((3 * D, TOK), BF16),
            pltpu.VMEM((D, 256), F32),
            pltpu.VMEM((reps // 2, HD + 8, 256), BF16),
            pltpu.VMEM((reps // 2, HD + 8, 256), BF16),
            pltpu.VMEM((reps // 2, HD + 8, 256), BF16),
            pltpu.VMEM((reps // 2, HD + 8, 256), BF16),
            pltpu.VMEM((VIEWS, ROWS, COLS, HD), BF16),
            pltpu.VMEM((TOK, D), BF16),
            pltpu.VMEM((D // reps, 3 * HD), F32),
            DMA((3,)),
            DMA((2,)),
            DMA((2,)),
            DMA((8,)),
            DMA((8,)),
            DMA((NZ, NX)),
            DMA((NZ, NX)),
            DMA((NZ, NX)),
            DMA((NZ, NX)),
            DMA((4,)),
            DMA((4,)),
            DMA((SEQS,)),
            DMA((SEQS,)),
            DMA((SEQS,)),
            DMA((SEQS,)),
            DMA,
            DMA,
            DMA((reps // 2,)),
            DMA((reps // 2,)),
        ],
        compiler_params=pltpu.CompilerParams(
            collective_id=0, has_side_effects=True, vmem_limit_bytes=62 * 2**20
        ),
        name="layer",
    )(
        features.reshape(TOK, depth),
        conv_weight.transpose(0, 1, 3, 2).reshape(9, 4, depth),
        conv_bias,
        noise.transpose(0, 1, 2, 4, 3).reshape(VIEWS, 4, COLS),
        timestep,
        camera,
        view_table,
        latent_proj,
        hidden.reshape(TOK, D),
        ln_gain,
        qkv_weight,
        cotangent.reshape(VIEWS, ROWS, COLS, HD),
    )
    att, hgrad, wgrad = pl.pallas_call(
        hand_out,
        out_shape=outs,
        in_specs=[ANY] * 3,
        out_specs=(pl.BlockSpec(memory_space=pltpu.VMEM),) * 3,
        scratch_shapes=[DMA((3,))],
        compiler_params=pltpu.CompilerParams(vmem_limit_bytes=62 * 2**20),
        name="hand_out",
    )(*results)
    return (
        att.reshape(cotangent.shape),
        hgrad.reshape(hidden.shape),
        wgrad.reshape(1, D // reps, 3 * HD),
    )


def solution(mesh):
    return jax.shard_map(
        on_device,
        mesh=mesh,
        in_specs=(
            P(("grp", "dp"), None, "seq", None, None),
            P(),
            P(),
            P(("grp", "dp"), None, "seq", None, None),
            P(("grp", "dp")),
            P(("grp", "dp"), None),
            P(),
            P(),
            P(("grp", "dp"), None, "seq", None, None),
            P(),
            P(),
            P(("grp", "dp"), None, None, None, "seq"),
        ),
        out_specs=(
            P(("grp", "dp"), None, None, None, "seq"),
            P(("grp", "dp"), None, "seq", None, None),
            P("seq", ("grp", "dp"), None),
        ),
        check_vma=False,
    )
```
